512 devices in a mesh: grp: 8 (over z_hi, y), seq: 8 (over x, core), tp: 8 (over z_lo).
Axes of the slice: x: 4, y: 4, z: 16 (z_hi: 2, z_lo: 8; z = z_hi * 8 + z_lo), core: 2. Of those that a mesh axis runs over, the one named last changes fastest.
Arguments:
- fc_big: bfloat16 [8192, 6912], P(('grp', 'seq'), 'tp'), may hold values from -6 to 6
- fc_guide: bfloat16 [8192, 4480], P(('grp', 'seq'), 'tp'), may hold values from -6 to 6
- res_big: bfloat16 [8192, 5120], P(('grp', 'tp'), 'seq'), may hold values from -6 to 6
- res_guide: bfloat16 [8192, 1536], P(('grp', 'tp'), 'seq'), may hold values from -6 to 6
- cotangent: float32 [8192, 64], P(('grp', 'tp')), may hold values from -6 to 6
- proj_big: bfloat16 [6912, 5120], P('tp', 'seq'), may hold values from -0.078125 to 0.078125
- proj_guide: bfloat16 [4480, 1536], P('tp', 'seq'), may hold values from -0.09375 to 0.09375
- head_big: bfloat16 [5120, 64], P('seq'), may hold values from -0.078125 to 0.078125
- head_guide: bfloat16 [1536, 64], P('seq'), may hold values from -0.15625 to 0.15625
- modulation_big: float32 [50, 3, 5120], P(None, None, 'seq'), may hold values from -3 to 3
- modulation_guide: float32 [50, 3, 1536], P(None, None, 'seq'), may hold values from -3 to 3
- weight_table: float32 [8], replicated, may hold values from 1.5 to 4
- time_index: int32 [8], P('grp'), may hold values from 0 to 49
- weight_index: int32 [8], P('grp'), may hold values from 0 to 7
Outputs:
- guided: float32 [8192, 64], P(('grp', 'tp'))
- grad_proj: bfloat16 [6912, 5120], P('tp', 'seq')
- grad_head: float32 [5120, 64], P('seq')
- grad_res_big: bfloat16 [8192, 5120], P(('grp', 'tp'), 'seq')
- grad_res_guide: bfloat16 [8192, 1536], P(('grp', 'tp'), 'seq')
The draws below stay inside these ranges and needn't reach their ends.
All inputs are finite; a program needn't handle non-finite values.
Results may differ from the reference program's by a relative error of at most 0.019.
Values may be sent and summed in bfloat16 or wider, within the bound.
A program may use at most 64 MiB of HBM per device.

```python
import jax
import jax.numpy as jnp
from jax import lax

DB = 5120
FFB = 6912
DG = 1536
FFG = 4480
PATCH = 64
STEPS = 50
LEVELS = 8
GROUP_TOKENS = 1024
TOKENS = 8192
SAMPLES = 8
N_GRP = 8
N_TP = 8


def touch_ends(drawn, rng, least, high):
    index_at = [jax.random.randint(jax.random.fold_in(rng, axis), (), 0, length) for axis, length in enumerate(drawn.shape)]
    widest = drawn.shape.index(max(drawn.shape))
    next_to = index_at[:widest] + [(index_at[widest] + 1) % drawn.shape[widest]] + index_at[widest + 1:]
    return drawn.at[tuple(index_at)].set(least).at[tuple(next_to)].set(high)


def levels(stream_key, dims, pieces, smallest, largest):
    loudness, own = 1.0, jax.random.fold_in(stream_key, 6)
    for dim, parts in pieces:
        steps = jnp.exp(jax.random.uniform(jax.random.fold_in(own, dim), (parts,), jnp.float32, smallest / len(pieces), largest / len(pieces)))
        loudness = loudness * jnp.repeat(steps, dims[dim] // parts).reshape([-1 if axis == dim else 1 for axis in range(len(dims))])
    return loudness


def normal_values(own_key, dims, width, bound, cuts=(), kind=jnp.bfloat16):
    drawn = width * jax.random.normal(own_key, dims, jnp.float32)
    if cuts:
        drawn = drawn * levels(own_key, dims, cuts, -0.22, 0.18)
    return jnp.clip(drawn, -bound, bound).astype(kind)


def setup_inputs(seed: int = 0) -> dict:
    splits = jax.random.split(jax.random.key(seed), 15)
    fc_big = normal_values(splits[0], (TOKENS, FFB), 1.0, 6.0, ((0, 64), (1, 8)))
    fc_guide = normal_values(splits[1], (TOKENS, FFG), 1.0, 6.0, ((0, 64), (1, 8)))
    res_big = normal_values(splits[2], (TOKENS, DB), 1.0, 6.0, ((0, 64), (1, 8)))
    res_guide = normal_values(splits[3], (TOKENS, DG), 1.0, 6.0, ((0, 64), (1, 8)))
    cotangent = normal_values(splits[4], (TOKENS, PATCH), 1.0, 6.0, ((0, 64),), jnp.float32)
    proj_big = normal_values(splits[5], (FFB, DB), FFB ** -0.5, 0.078125, ((0, 8), (1, 8)))
    proj_guide = normal_values(splits[6], (FFG, DG), FFG ** -0.5, 0.09375, ((0, 8), (1, 8)))
    head_big = normal_values(splits[7], (DB, PATCH), DB ** -0.5, 0.078125, ((0, 8),))
    head_guide = normal_values(splits[8], (DG, PATCH), DG ** -0.5, 0.15625, ((0, 8),))
    modulation_big = normal_values(splits[9], (STEPS, 3, DB), 0.5, 3.0, ((2, 8),), jnp.float32)
    modulation_guide = normal_values(splits[10], (STEPS, 3, DG), 0.5, 3.0, ((2, 8),), jnp.float32)
    weight_table = jnp.clip(jax.random.uniform(splits[11], (LEVELS,), jnp.float32, 1.5, 4.0), 1.5, 4.0)
    time_index = touch_ends(jax.random.randint(splits[12], (SAMPLES,), 0, STEPS), jax.random.fold_in(splits[12], 1), 0, STEPS - 1).astype(jnp.int32)
    weight_index = touch_ends(jax.random.randint(splits[13], (SAMPLES,), 0, LEVELS), jax.random.fold_in(splits[13], 1), 0, LEVELS - 1).astype(jnp.int32)
    return dict(fc_big=fc_big, fc_guide=fc_guide, res_big=res_big, res_guide=res_guide, cotangent=cotangent, proj_big=proj_big, proj_guide=proj_guide, head_big=head_big, head_guide=head_guide, modulation_big=modulation_big, modulation_guide=modulation_guide, weight_table=weight_table, time_index=time_index, weight_index=weight_index)


EPSILON = 1e-06

def split_sum(hidden, weight):
    stride = weight.shape[0] // N_TP
    running = jnp.zeros((hidden.shape[0], weight.shape[1]), jnp.float32)
    for segment in range(N_TP):
        portion = jnp.dot(hidden[:, segment * stride:(segment + 1) * stride], weight[segment * stride:(segment + 1) * stride], preferred_element_type=jnp.float32)
        rounded = lax.optimization_barrier(portion.astype(jnp.bfloat16))
        running = running + rounded.astype(jnp.float32)
    return running

def forward_model(hidden, stream_in, weight, table_row):
    summed = split_sum(hidden, weight)
    stream = stream_in.astype(jnp.float32) + table_row[0] * summed
    centre = lax.optimization_barrier(jnp.mean(stream, axis=1, keepdims=True))
    centred = stream - centre
    variance = lax.optimization_barrier(jnp.mean(centred * centred, axis=1, keepdims=True))
    inverse_std = lax.rsqrt(variance + EPSILON)
    normed = centred * inverse_std
    shaped = (normed * (1.0 + table_row[2]) + table_row[1]).astype(jnp.bfloat16)
    return (normed, inverse_std, shaped)

def backward_norm(cot_rows, head, table_row, normed, inverse_std):
    upstream = jnp.dot(cot_rows, head.T, preferred_element_type=jnp.float32)
    scaled = upstream * (1.0 + table_row[2])
    first_mean = lax.optimization_barrier(jnp.mean(scaled, axis=1, keepdims=True))
    second_mean = lax.optimization_barrier(jnp.mean(scaled * normed, axis=1, keepdims=True))
    return inverse_std * (scaled - first_mean - normed * second_mean)

def reference(fc_big, fc_guide, res_big, res_guide, cotangent, proj_big, proj_guide, head_big, head_guide, modulation_big, modulation_guide, weight_table, time_index, weight_index):

    def sample_step(running, sample_slices):
        hidden_big, hidden_guide, stream_big, stream_guide, cotangent_rows, time_value, level_value = sample_slices
        strength = weight_table[level_value]
        table_big = modulation_big[time_value]
        table_guide = modulation_guide[time_value]
        normed_big, inverse_big, shaped_big = forward_model(hidden_big, stream_big, proj_big, table_big)
        normed_guide, inverse_guide, shaped_guide = forward_model(hidden_guide, stream_guide, proj_guide, table_guide)
        out_big = jnp.dot(shaped_big, head_big, preferred_element_type=jnp.float32)
        out_guide = jnp.dot(shaped_guide, head_guide, preferred_element_type=jnp.float32)
        guided_rows = out_guide + strength * (out_big - out_guide)
        cot_big = (strength * cotangent_rows).astype(jnp.bfloat16)
        cot_guide = ((1.0 - strength) * cotangent_rows).astype(jnp.bfloat16)
        grad_big = backward_norm(cot_big, head_big, table_big, normed_big, inverse_big)
        grad_guide = backward_norm(cot_guide, head_guide, table_guide, normed_guide, inverse_guide)
        signal = (grad_big * table_big[0]).astype(jnp.bfloat16)
        proj_part = jnp.dot(hidden_big.T, signal, preferred_element_type=jnp.float32)
        head_part = jnp.dot(shaped_big.T, cot_big, preferred_element_type=jnp.float32)
        return ((running[0] + proj_part, running[1] + head_part), (guided_rows, grad_big.astype(jnp.bfloat16), grad_guide.astype(jnp.bfloat16)))
    sample_slices = (fc_big.reshape(N_GRP, GROUP_TOKENS, FFB), fc_guide.reshape(N_GRP, GROUP_TOKENS, FFG), res_big.reshape(N_GRP, GROUP_TOKENS, DB), res_guide.reshape(N_GRP, GROUP_TOKENS, DG), cotangent.reshape(N_GRP, GROUP_TOKENS, PATCH), time_index, weight_index)
    initial = (jnp.zeros((FFB, DB), jnp.float32), jnp.zeros((DB, PATCH), jnp.float32))
    totals, stacked = lax.scan(sample_step, initial, sample_slices)
    guided = stacked[0].reshape(TOKENS, PATCH)
    grad_res_big = stacked[1].reshape(TOKENS, DB)
    grad_res_guide = stacked[2].reshape(TOKENS, DG)
    return (guided, totals[0].astype(jnp.bfloat16), totals[1], grad_res_big, grad_res_guide)
```

```python
import jax
import jax.numpy as jnp
from jax import lax
from jax.experimental import pallas as pl
from jax.experimental.pallas import tpu as pltpu
from jax.sharding import PartitionSpec as P

MESH = pl.DeviceIdType.MESH
F32 = jnp.float32
BF16 = jnp.bfloat16

DB = 5120
DG = 1536
EPSILON = 1e-06

TOK = 128
WB = 640
WG = 192
HB = 864
HBP = 896
HG = 560
HGP = 640
FLAT = 832
NQ = 4
SUB = FLAT // NQ
SKEW = 3
NA = 4
ASUB = WB // NA
NC = 5
SHARD = 224
HALF = 112


def remote(src, dst, send, recv, device):
    return pltpu.make_async_remote_copy(
        src_ref=src, dst_ref=dst, send_sem=send, recv_sem=recv, device_id=device, device_id_type=MESH
    )


def kernel(
    time_ref,
    level_ref,
    table_ref,
    fc_b,
    fc_g,
    res_b,
    res_g,
    cot_ref,
    proj_b_hbm,
    proj_g_hbm,
    head_b,
    head_g,
    mod_b,
    mod_g,
    guided_ref,
    grad_proj_hbm,
    grad_head_ref,
    grad_res_b,
    grad_res_g,
    proj_b,
    proj_g,
    fc_all,
    fc_t,
    term,
    got_r,
    got_l,
    put_r,
    put_l,
    total,
    dev_b,
    dev_g,
    scaled_b,
    scaled_g,
    spread,
    cots,
    cot_t,
    stats,
    facts,
    signal,
    shaped,
    head_sum,
    parts,
    grad,
    one_a,
    one_b,
    two_a,
    two_b,
    mid_a,
    mid_b,
    zed,
    zed_in,
    final,
    heads,
    head_full,
    local_sem,
    fc_send,
    fc_recv,
    cot_send,
    cot_recv,
    r_send,
    r_recv,
    l_send,
    l_recv,
    ar_send,
    al_send,
    a_recv,
    st_send,
    st_recv,
    fa_send,
    fa_recv,
    pt_send,
    pt_recv,
    one_send,
    one_recv,
    two_send,
    two_recv,
    z_send,
    z_recv,
    g1_send,
    g1_recv,
    g2_send,
    g2_recv,
    hd_send,
    hd_recv,
    out_sem,
):
    grp = lax.axis_index("grp")
    me = lax.axis_index("seq")
    j = lax.axis_index("tp")
    y = lax.rem(grp, 4)
    zh4 = grp - y
    x = lax.div(me, 2)
    core = lax.rem(me, 2)
    y_flip = y + 1 - 2 * lax.rem(y, 2)
    y_back = 3 - y
    sib = me + 1 - 2 * core
    xr = lax.rem(x + 1, 4)
    xl = lax.rem(x + 3, 4)
    xf = lax.rem(x + 2, 4)
    dev_flip = {"grp": zh4 + y_flip}
    dev_back = {"grp": zh4 + y_back}
    dev_z = {"grp": lax.rem(grp + 4, 8)}

    def seq_peer(n):
        return lax.rem(me + n, 8)

    def tp_peer(n):
        return lax.rem(j + n, 8)

    barrier = pltpu.get_barrier_semaphore()
    for n in range(1, 8):
        pl.semaphore_signal(barrier, inc=1, device_id={"seq": seq_peer(n)}, device_id_type=MESH)
        pl.semaphore_signal(barrier, inc=1, device_id={"tp": tp_peer(n)}, device_id_type=MESH)
    for device in (dev_flip, dev_back, dev_z):
        pl.semaphore_signal(barrier, inc=1, device_id=device, device_id_type=MESH)

    load_b = pltpu.make_async_copy(proj_b_hbm, proj_b.at[pl.ds(0, HB)], local_sem.at[0])
    load_g = pltpu.make_async_copy(proj_g_hbm, proj_g.at[pl.ds(0, HG)], local_sem.at[1])
    load_b.start()
    load_g.start()
    proj_b[HB:HBP, :] = jnp.zeros((HBP - HB, WB), BF16)
    proj_g[HG:HGP, :] = jnp.zeros((HGP - HG, WG), BF16)
    fc_all[me, :, 0:HBP] = jnp.concatenate([fc_b[...], jnp.zeros((TOK, HBP - HB), BF16)], axis=1)
    fc_all[me, :, HBP : HBP + HGP] = jnp.concatenate(
        [fc_g[...], jnp.zeros((TOK, HGP - HG), BF16)], axis=1
    )
    strength = table_ref[level_ref[0]]
    when = time_ref[0]
    rows_b = mod_b[when]
    rows_g = mod_g[when]
    gate_b, shift_b, scale_b = rows_b[0:1], rows_b[1:2], 1.0 + rows_b[2:3]
    gate_g, shift_g, scale_g = rows_g[0:1], rows_g[1:2], 1.0 + rows_g[2:3]
    cot = cot_ref[...]
    cot_b = (strength * cot).astype(BF16)
    cot_g = ((1.0 - strength) * cot).astype(BF16)
    cots[j] = jnp.concatenate([cot_b[0:64], cot_b[64:128]], axis=1)
    pl.semaphore_wait(barrier, 17)

    def hidden(s, h):
        return fc_all.at[s, pl.ds(64 * h, 64)]

    def hidden_copy(s, h, k, target):
        return remote(hidden(s, h), hidden(s, h), fc_send.at[k], fc_recv.at[s, h], {"seq": target})

    to_r, to_l = 2 * xr + core, 2 * xl + core
    sent = []

    def send_hidden(s, h, k, target):
        copy = hidden_copy(s, h, k, target)
        copy.start()
        sent.append(copy)

    def wait_hidden(s, h):
        hidden_copy(s, h, 0, sib).wait_recv()

    send_hidden(me, 0, 0, to_r)
    send_hidden(me, 1, 1, to_l)
    send_hidden(me, 0, 2, sib)
    send_hidden(me, 1, 3, sib)
    send_hidden(me, 1, 4, to_r)
    send_hidden(me, 0, 5, to_l)

    for n in range(1, 8):
        p = tp_peer(n)
        copy = remote(cots.at[j], cots.at[j], cot_send.at[n], cot_recv.at[j], {"tp": p})
        copy.start()
        sent.append(copy)

    scaled_b[...] = (
        lax.dot_general(cot_b, head_b[...], (((1,), (1,)), ((), ())), preferred_element_type=F32)
        * scale_b
    )
    scaled_g[...] = (
        lax.dot_general(cot_g, head_g[...], (((1,), (1,)), ((), ())), preferred_element_type=F32)
        * scale_g
    )
    load_b.wait()
    load_g.wait()

    def terms(first, second):
        def one(i, carry):
            s = jnp.where(i == 0, first, second)
            block = fc_all[s, :, 0:HBP]
            product = jnp.dot(block, proj_b[...], preferred_element_type=F32)
            for q in range(NC):
                term[s, pl.ds(128 * q, 128), :] = product[:, 128 * q : 128 * q + 128]
            product = jnp.dot(
                fc_all[s, :, HBP : HBP + HGP], proj_g[...], preferred_element_type=F32
            )
            term[s, 640:768, :] = product[:, 0:128]
            term[s, 768:832, :] = jnp.concatenate(
                [product[0:64, 128:192], product[64:128, 128:192]], axis=1
            )
            fc_t[:, pl.ds(pl.multiple_of(s * 128, 128), 128)] = block.T
            return carry

        lax.fori_loop(0, 2, one, 0)

    left, right, far = to_l, to_r, 2 * xf + core
    left_s, right_s, far_s = 2 * xl + 1 - core, 2 * xr + 1 - core, 2 * xf + 1 - core
    wait_hidden(sib, 0)
    wait_hidden(sib, 1)
    terms(me, sib)
    wait_hidden(left, 0)
    send_hidden(left, 0, 6, to_r)
    send_hidden(left, 0, 7, sib)
    wait_hidden(right, 1)
    send_hidden(right, 1, 8, to_l)
    send_hidden(right, 1, 9, sib)
    wait_hidden(left, 1)
    send_hidden(left, 1, 10, sib)
    wait_hidden(right, 0)
    send_hidden(right, 0, 11, sib)
    terms(left, right)
    for h in range(2):
        wait_hidden(left_s, h)
        wait_hidden(right_s, h)
    terms(left_s, right_s)
    wait_hidden(far, 0)
    send_hidden(far, 0, 12, sib)
    wait_hidden(far, 1)
    send_hidden(far, 1, 13, sib)
    wait_hidden(far_s, 0)
    wait_hidden(far_s, 1)
    terms(far, far_s)

    def piece(q):
        return pl.ds(pl.multiple_of(q * SUB, 16), SUB)

    def sum_copy(right_way, i, q):
        if right_way:
            return remote(
                put_r.at[i, piece(q)], got_r.at[i, piece(q)], r_send.at[i, q], r_recv.at[i, q], {"tp": j + 1}
            )
        return remote(
            put_l.at[i, piece(q)], got_l.at[i, piece(q)], l_send.at[i, q], l_recv.at[i, q], {"tp": j - 1}
        )

    def tick(t, carry):
        for right_way in (True, False):
            place = j if right_way else 7 - j
            u = t - SKEW * place
            put, got = (put_r, got_r) if right_way else (put_l, got_l)

            @pl.when((u >= 0) & (u < (7 - place) * NQ))
            def _():
                i = lax.div(u, NQ)
                q = lax.rem(u, NQ)
                d = 7 - i if right_way else i
                own = term[d, piece(q), :]

                @pl.when(place > 0)
                def _():
                    sum_copy(right_way, i, q).wait_recv()
                    put[i, piece(q), :] = (got[i, piece(q), :].astype(F32) + own).astype(BF16)

                @pl.when(place == 0)
                def _():
                    put[i, piece(q), :] = own.astype(BF16)

                sum_copy(right_way, i, q).start()

        return carry

    lax.fori_loop(0, 7 * NQ + 7 * SKEW, tick, 0)

    total[...] = term[j]
    for right_way in (True, False):
        place = j if right_way else 7 - j
        got = got_r if right_way else got_l

        @pl.when(place > 0)
        def _():
            for q in range(NQ):
                sum_copy(right_way, 7 - place, q).wait_recv()
            total[...] += got[7 - place].astype(F32)

    summed_b = jnp.concatenate([total[128 * q : 128 * q + 128, :] for q in range(NC)], axis=1)
    stream_b = res_b[...].astype(F32) + gate_b * summed_b
    mean_b = jnp.sum(stream_b, axis=1, keepdims=True) * (1.0 / WB)
    away_b = stream_b - mean_b
    for q in range(NC):
        spread[j, 128 * q : 128 * q + 128, :] = away_b[:, 128 * q : 128 * q + 128].astype(BF16)
    dev_b[...] = away_b

    def a_piece(q):
        return pl.ds(q * ASUB, ASUB)

    def a_copy(right_way, k, q):
        if right_way:
            return remote(
                spread.at[k, a_piece(q)], spread.at[k, a_piece(q)], ar_send.at[k, q], a_recv.at[k, q], {"tp": j + 1}
            )
        return remote(
            spread.at[k, a_piece(q)], spread.at[k, a_piece(q)], al_send.at[k, q], a_recv.at[k, q], {"tp": j - 1}
        )

    def forward(i):
        for q in range(NA):
            for right_way in (True, False):
                place = j if right_way else 7 - j
                k = j - i if right_way else j + i

                @pl.when(place >= i)
                def _():
                    @pl.when(i > 0)
                    def _():
                        a_copy(right_way, k, q).wait_recv()

                    @pl.when(place < 7)
                    def _():
                        a_copy(right_way, k, q).start()

    forward(jnp.int32(0))

    tail_g = total[768:832, :]
    summed_g = jnp.concatenate(
        [total[640:768, :], jnp.concatenate([tail_g[:, 0:64], tail_g[:, 64:128]], axis=0)], axis=1
    )
    stream_g = res_g[...].astype(F32) + gate_g * summed_g
    mean_g = jnp.sum(stream_g, axis=1, keepdims=True) * (1.0 / WG)
    away_g = stream_g - mean_g
    dev_g[...] = away_g
    up_b, up_g = scaled_b[...], scaled_g[...]
    columns = (
        mean_b,
        jnp.sum(away_b * away_b, axis=1, keepdims=True),
        jnp.sum(up_b, axis=1, keepdims=True),
        jnp.sum(up_b * away_b, axis=1, keepdims=True),
        mean_g,
        jnp.sum(away_g * away_g, axis=1, keepdims=True),
        jnp.sum(up_g, axis=1, keepdims=True),
        jnp.sum(up_g * away_g, axis=1, keepdims=True),
    )
    lane = lax.broadcasted_iota(jnp.int32, (TOK, 128), 1)
    square = jnp.zeros((TOK, 128), F32)
    for n, column in enumerate(columns):
        square = jnp.where(lane == n, column, square)
    stats[me] = square.T[0:8]
    for n in range(1, 8):
        copy = remote(stats.at[me], stats.at[me], st_send.at[n], st_recv.at[me], {"seq": seq_peer(n)})
        copy.start()
        sent.append(copy)

    forward(jnp.int32(1))

    for n in range(1, 8):
        p = tp_peer(n)
        remote(cots.at[p], cots.at[p], cot_send.at[0], cot_recv.at[p], {"tp": p}).wait_recv()
    for n in range(1, 8):
        p = seq_peer(n)
        remote(stats.at[p], stats.at[p], st_send.at[0], st_recv.at[p], {"seq": p}).wait_recv()

    mine = stats[me]

    def norm(base, width, whole):
        every = [stats[s] for s in range(8)]
        centre = sum(r[base : base + 1] for r in every) * (1.0 / 8)
        gaps = [r[base : base + 1] - centre for r in every]
        square_sum = sum(r[base + 1 : base + 2] + width * (g * g) for r, g in zip(every, gaps))
        inverse = lax.rsqrt(square_sum * (1.0 / whole) + EPSILON)
        first = sum(r[base + 2 : base + 3] for r in every) * (1.0 / whole)
        cross = sum(r[base + 3 : base + 4] + r[base + 2 : base + 3] * g for r, g in zip(every, gaps))
        second = inverse * cross * (1.0 / whole)
        offset = inverse * (mine[base : base + 1] - centre)
        return inverse, offset, inverse * inverse * second, inverse * (first + offset * second)

    norm_b = norm(0, float(WB), float(DB))
    norm_g = norm(4, float(WG), float(DG))
    facts[j] = jnp.concatenate(norm_b + norm_g, axis=0)
    for n in range(1, 8):
        copy = remote(facts.at[j], facts.at[j], fa_send.at[n], fa_recv.at[j], {"tp": tp_peer(n)})
        copy.start()
        sent.append(copy)

    def as_columns(rows):
        return jnp.concatenate([rows, jnp.zeros((120, 128), F32)], axis=0).T

    head_sum[...] = jnp.zeros_like(head_sum)

    def consume(k):
        @pl.when(k != j)
        def _():
            remote(facts.at[k], facts.at[k], fa_send.at[0], fa_recv.at[k], {"tp": k}).wait_recv()

        turned = as_columns(facts[k])
        inverse, offset, slope, base = (turned[:, n : n + 1] for n in range(4))
        packed = cots[k].astype(F32)
        cot_k = jnp.concatenate([packed[:, 0:64], packed[:, 64:128]], axis=0)
        up = lax.dot_general(
            cot_k.astype(BF16), head_b[...], (((1,), (1,)), ((), ())), preferred_element_type=F32
        )
        away = jnp.concatenate(
            [spread[k, 128 * q : 128 * q + 128, :] for q in range(NC)], axis=1
        ).astype(F32)
        signal[pl.ds(pl.multiple_of(k * 128, 128), 128), :] = (
            gate_b * (inverse * (up * scale_b) - slope * away - base)
        ).astype(BF16)
        shaped_k = ((inverse * away + offset) * scale_b + shift_b).astype(BF16)
        shaped[...] = shaped_k
        head_sum[...] += jnp.dot(
            cot_k.T.astype(BF16), shaped_k, preferred_element_type=F32
        )

    def consume_both(i):
        @pl.when(j >= i)
        def _():
            consume(j - i)

        @pl.when((j + i <= 7) & (i > 0))
        def _():
            consume(j + i)

    def step(i, carry):
        @pl.when(i < 8)
        def _():
            forward(i)

        consume_both(i - 2)
        return carry

    lax.fori_loop(2, 10, step, 0)

    def rows(shard, half):
        return pl.ds(pl.multiple_of(shard * SHARD + half * HALF, 16), HALF)

    def one_copies(c):
        return [
            remote(grad.at[c, rows(y_flip, 0)], one_a.at[c, 0], one_send.at[c, 0], one_recv.at[c, 0], dev_flip),
            remote(grad.at[c, rows(3 - y_flip, 0)], one_a.at[c, 1], one_send.at[c, 1], one_recv.at[c, 1], dev_flip),
            remote(grad.at[c, rows(y_back, 1)], one_b.at[c, 0], one_send.at[c, 2], one_recv.at[c, 2], dev_back),
            remote(grad.at[c, rows(3 - y_flip, 1)], one_b.at[c, 1], one_send.at[c, 3], one_recv.at[c, 3], dev_back),
        ]

    def two_copies(c):
        return [
            remote(mid_a.at[c, 1], two_a.at[c], two_send.at[c, 0], two_recv.at[c, 0], dev_back),
            remote(mid_b.at[c, 1], two_b.at[c], two_send.at[c, 1], two_recv.at[c, 1], dev_flip),
        ]

    def z_copy(c):
        return remote(zed.at[c], zed_in.at[c], z_send.at[c], z_recv.at[c], dev_z)

    def back_one(c):
        a, b = final.at[c, rows(y, 0)], final.at[c, rows(y, 1)]
        return [
            remote(a, a, g1_send.at[c, 0], g1_recv.at[c, 0], dev_back),
            remote(b, b, g1_send.at[c, 1], g1_recv.at[c, 1], dev_flip),
        ]

    def back_two(c):
        shards = [(y, 0, dev_flip), (y_back, 0, dev_flip), (y, 1, dev_back), (y_flip, 1, dev_back)]
        out = []
        for n, (shard, half, device) in enumerate(shards):
            ref = final.at[c, rows(shard, half)]
            out.append(remote(ref, ref, g2_send.at[c, n], g2_recv.at[c, n], device))
        return out

    def add(a, b):
        return (a.astype(F32) + b.astype(F32)).astype(BF16)

    patch_rows = head_sum[pl.ds(pl.multiple_of(j * 8, 8), 8), :]
    spare = [patch_rows[:, 128 * q : 128 * q + 128] for q in range(NC)]
    spare = [
        jnp.concatenate(spare[0:4], axis=0),
        jnp.concatenate([spare[4], jnp.zeros((24, 128), F32)], axis=0),
    ]
    for t in range(NC + 2):
        if t < NC:
            c = t
            grad[c] = jnp.dot(
                fc_t[...], signal[:, 128 * c : 128 * c + 128], preferred_element_type=F32
            ).astype(BF16)
            if c < 2:
                grad[c, HB:HBP, :] = spare[c].astype(BF16)
            for copy in one_copies(c):
                copy.start()
                sent.append(copy)
        if 0 <= t - 1 < NC:
            c = t - 1
            for copy in one_copies(c):
                copy.wait_recv()
            mid_a[c, 0] = add(grad[c, rows(y, 0), :], one_a[c, 0])
            mid_a[c, 1] = add(grad[c, rows(y_back, 0), :], one_a[c, 1])
            mid_b[c, 0] = add(grad[c, rows(y, 1), :], one_b[c, 0])
            mid_b[c, 1] = add(grad[c, rows(y_flip, 1), :], one_b[c, 1])
            for copy in two_copies(c):
                copy.start()
                sent.append(copy)
        if 0 <= t - 2 < NC:
            c = t - 2
            for copy in two_copies(c):
                copy.wait_recv()
            zed[c, 0:HALF, :] = add(mid_a[c, 0], two_a[c])
            zed[c, HALF:SHARD, :] = add(mid_b[c, 0], two_b[c])
            copy = z_copy(c)
            copy.start()
            sent.append(copy)

    turned = as_columns(facts[j])
    inv_b, off_b, slope_b, base_b, inv_g, off_g, slope_g, base_g = (turned[:, n : n + 1] for n in range(8))
    grad_res_b[...] = (inv_b * scaled_b[...] - slope_b * dev_b[...] - base_b).astype(BF16)
    grad_res_g[...] = (inv_g * scaled_g[...] - slope_g * dev_g[...] - base_g).astype(BF16)
    shaped_b = ((inv_b * dev_b[...] + off_b) * scale_b + shift_b).astype(BF16)
    shaped_g = ((inv_g * dev_g[...] + off_g) * scale_g + shift_g).astype(BF16)
    part = strength * jnp.dot(shaped_b, head_b[...], preferred_element_type=F32) + (
        1.0 - strength
    ) * jnp.dot(shaped_g, head_g[...], preferred_element_type=F32)
    parts[me] = jnp.concatenate([part[0:64], part[64:128]], axis=1).astype(BF16)
    for n in range(1, 8):
        copy = remote(parts.at[me], parts.at[me], pt_send.at[n], pt_recv.at[me], {"seq": seq_peer(n)})
        copy.start()
        sent.append(copy)

    outs = []
    for t in range(NC + 2):
        if t < NC:
            c = t
            z_copy(c).wait_recv()
            final[c, pl.ds(pl.multiple_of(y * SHARD, 16), SHARD), :] = add(zed[c], zed_in[c])
            for copy in back_one(c):
                copy.start()
                sent.append(copy)
        if 0 <= t - 1 < NC:
            c = t - 1
            for copy in back_one(c):
                copy.wait_recv()
            for copy in back_two(c):
                copy.start()
                sent.append(copy)
        if 0 <= t - 2 < NC:
            c = t - 2
            for copy in back_two(c):
                copy.wait_recv()
            copy = pltpu.make_async_copy(
                final.at[c, pl.ds(0, HB)], grad_proj_hbm.at[:, pl.ds(128 * c, 128)], out_sem.at[c]
            )
            copy.start()
            outs.append(copy)
            if c == 1:
                heads[j, 0:32, :] = final[0, HB:HBP, :]
                heads[j, 32:64, :] = final[1, HB:HBP, :]
                for n in range(1, 8):
                    copy = remote(
                        heads.at[j], heads.at[j], hd_send.at[n], hd_recv.at[j], {"tp": tp_peer(n)}
                    )
                    copy.start()
                    sent.append(copy)
        if t == NC - 1:
            for n in range(1, 8):
                p = seq_peer(n)
                remote(parts.at[p], parts.at[p], pt_send.at[0], pt_recv.at[p], {"seq": p}).wait_recv()
            whole = sum(parts[s].astype(F32) for s in range(8))
            guided_ref[...] = jnp.concatenate([whole[:, 0:64], whole[:, 64:128]], axis=0)

    for n in range(1, 8):
        p = tp_peer(n)
        remote(heads.at[p], heads.at[p], hd_send.at[0], hd_recv.at[p], {"tp": p}).wait_recv()
    for p in range(8):
        block = heads[p].astype(F32)
        for q in range(NC):
            head_full[8 * p : 8 * p + 8, 128 * q : 128 * q + 128] = block[8 * q : 8 * q + 8]
    for q in range(NC):
        grad_head_ref[128 * q : 128 * q + 128, :] = head_full[:, 128 * q : 128 * q + 128].T

    for copy in outs:
        copy.wait()
    for copy in sent:
        copy.wait_send()

    def drain(t, carry):
        i = lax.div(t, NQ)
        q = lax.rem(t, NQ)
        for right_way in (True, False):
            place = j if right_way else 7 - j

            @pl.when(i < 7 - place)
            def _():
                sum_copy(right_way, i, q).wait_send()

        return carry

    lax.fori_loop(0, 7 * NQ, drain, 0)

    def drain_all(i, carry):
        for right_way in (True, False):
            place = j if right_way else 7 - j
            k = j - i if right_way else j + i

            @pl.when((place >= i) & (place < 7))
            def _():
                for q in range(NA):
                    a_copy(right_way, k, q).wait_send()

        return carry

    lax.fori_loop(0, 8, drain_all, 0)


def shards(
    fc_big,
    fc_guide,
    res_big,
    res_guide,
    cotangent,
    proj_big,
    proj_guide,
    head_big,
    head_guide,
    modulation_big,
    modulation_guide,
    weight_table,
    time_index,
    weight_index,
):
    smem = pl.BlockSpec(memory_space=pltpu.SMEM)
    vmem = pl.BlockSpec(memory_space=pltpu.VMEM)
    hbm = pl.BlockSpec(memory_space=pl.ANY)
    dma = pltpu.SemaphoreType.DMA
    V = pltpu.VMEM
    return pl.pallas_call(
        kernel,
        out_shape=(
            jax.ShapeDtypeStruct((TOK, 64), F32),
            jax.ShapeDtypeStruct((HB, WB), BF16),
            jax.ShapeDtypeStruct((WB, 64), F32),
            jax.ShapeDtypeStruct((TOK, WB), BF16),
            jax.ShapeDtypeStruct((TOK, WG), BF16),
        ),
        in_specs=[smem, smem, smem, vmem, vmem, vmem, vmem, vmem, hbm, hbm, vmem, vmem, vmem, vmem],
        out_specs=(vmem, hbm, vmem, vmem, vmem),
        scratch_shapes=[
            V((HBP, WB), BF16),
            V((HGP, WG), BF16),
            V((8, TOK, HBP + HGP), BF16),
            V((HBP, 1024), BF16),
            V((8, FLAT, 128), F32),
            V((7, FLAT, 128), BF16),
            V((7, FLAT, 128), BF16),
            V((7, FLAT, 128), BF16),
            V((7, FLAT, 128), BF16),
            V((FLAT, 128), F32),
            V((TOK, WB), F32),
            V((TOK, WG), F32),
            V((TOK, WB), F32),
            V((TOK, WG), F32),
            V((8, WB, 128), BF16),
            V((8, 64, 128), BF16),
            V((64, 128), BF16),
            V((8, 8, 128), F32),
            V((8, 8, 128), F32),
            V((1024, WB), BF16),
            V((TOK, WB), BF16),
            V((64, WB), F32),
            V((8, 64, 128), BF16),
            V((NC, HBP, 128), BF16),
            V((NC, 2, HALF, 128), BF16),
            V((NC, 2, HALF, 128), BF16),
            V((NC, HALF, 128), BF16),
            V((NC, HALF, 128), BF16),
            V((NC, 2, HALF, 128), BF16),
            V((NC, 2, HALF, 128), BF16),
            V((NC, SHARD, 128), BF16),
            V((NC, SHARD, 128), BF16),
            V((NC, HBP, 128), BF16),
            V((8, 64, 128), BF16),
            V((64, WB), F32),
            dma((2,)),
            dma((14,)),
            dma((8, 2)),
            dma((8,)),
            dma((8,)),
            dma((7, NQ)),
            dma((7, NQ)),
            dma((7, NQ)),
            dma((7, NQ)),
            dma((8, NA)),
            dma((8, NA)),
            dma((8, NA)),
            dma((8,)),
            dma((8,)),
            dma((8,)),
            dma((8,)),
            dma((8,)),
            dma((8,)),
            dma((NC, 4)),
            dma((NC, 4)),
            dma((NC, 2)),
            dma((NC, 2)),
            dma((NC,)),
            dma((NC,)),
            dma((NC, 2)),
            dma((NC, 2)),
            dma((NC, 4)),
            dma((NC, 4)),
            dma((8,)),
            dma((8,)),
            dma((NC,)),
        ],
        compiler_params=pltpu.CompilerParams(
            collective_id=0, has_side_effects=True, vmem_limit_bytes=56 * 2**20
        ),
    )(
        time_index,
        weight_index,
        weight_table,
        fc_big,
        fc_guide,
        res_big,
        res_guide,
        cotangent,
        proj_big,
        proj_guide,
        head_big,
        head_guide,
        modulation_big,
        modulation_guide,
    )


def solution(mesh):
    placed = (
        P(("grp", "seq"), "tp"),
        P(("grp", "seq"), "tp"),
        P(("grp", "tp"), "seq"),
        P(("grp", "tp"), "seq"),
        P(("grp", "tp"), None),
        P("tp", "seq"),
        P("tp", "seq"),
        P("seq", None),
        P("seq", None),
        P(None, None, "seq"),
        P(None, None, "seq"),
        P(),
        P("grp"),
        P("grp"),
    )
    return jax.shard_map(
        shards,
        mesh=mesh,
        in_specs=placed,
        out_specs=(
            P(("grp", "tp"), None),
            P("tp", "seq"),
            P("seq", None),
            P(("grp", "tp"), "seq"),
            P(("grp", "tp"), "seq"),
        ),
        check_vma=False,
    )
```

```python
import jax
import jax.numpy as jnp
from jax import lax
from jax.experimental import pallas as pl
from jax.experimental.pallas import tpu as pltpu
from jax.sharding import PartitionSpec as P

MESH = pl.DeviceIdType.MESH
F32 = jnp.float32
BF16 = jnp.bfloat16

DB = 5120
DG = 1536
EPSILON = 1e-06

TOK = 128
WB = 640
WG = 192
HB = 864
HBP = 896
HG = 560
HGP = 640
PATCH = 64
STEPS = 50
NQ = 5
SUB = WB // NQ
UNITS = 8 * NQ
SKEW = 6
GSTEP = 2
NC = 5
SHARD = 224


def remote(src, dst, send, recv, device):
    return pltpu.make_async_remote_copy(
        src_ref=src, dst_ref=dst, send_sem=send, recv_sem=recv, device_id=device, device_id_type=MESH
    )


def kernel(
    time_ref,
    level_ref,
    table_ref,
    fc_b,
    fc_g,
    res_b_in,
    res_g_in,
    cot_in,
    proj_b_in,
    proj_g_in,
    head_b_in,
    head_g_in,
    mod_b_in,
    mod_g_in,
    guided_ref,
    grad_proj_ref,
    grad_head_ref,
    grad_res_b,
    grad_res_g,
    res_b,
    res_g,
    cot_ref,
    proj_b,
    proj_g,
    head_b,
    head_g,
    mod_b,
    mod_g,
    proj_bt,
    proj_gp,
    head_bt,
    gate_b,
    shift_b,
    scale_b,
    gate_g,
    shift_g,
    scale_g,
    fc_all,
    fcg_all,
    term,
    term_g,
    got,
    put,
    cross,
    means,
    gotg_r,
    gotg_l,
    putg_r,
    putg_l,
    dev_b,
    dev_g,
    scaled_b,
    scaled_g,
    spread,
    cots,
    stats,
    stats_g,
    facts,
    signal,
    head_sum,
    parts,
    grad,
    ones,
    zed,
    zed_in,
    final,
    heads,
    made_b,
    in_sem,
    fc_send,
    fc_recv,
    fcg_send,
    fcg_recv,
    cot_send,
    cot_recv,
    mn_send,
    mn_recv,
    in_send,
    in_recv,
    cross_recv,
    out_send,
    out_recv,
    rg_send,
    rg_recv,
    lg_send,
    lg_recv,
    st_send,
    st_recv,
    sg_send,
    sg_recv,
    pt_send,
    pt_recv,
    one_send,
    one_recv,
    z_send,
    z_recv,
    g1_send,
    g1_recv,
    hd_send,
    hd_recv,
):
    grp = lax.axis_index("grp")
    me = lax.axis_index("seq")
    j = lax.axis_index("tp")
    y = lax.rem(grp, 4)
    zh4 = grp - y
    x = lax.div(me, 2)
    core = lax.rem(me, 2)
    sib = me + 1 - 2 * core
    xr = lax.rem(x + 1, 4)
    xl = lax.rem(x + 3, 4)
    xf = lax.rem(x + 2, 4)
    dev_z = {"grp": lax.rem(grp + 4, 8)}

    def seq_peer(n):
        return lax.rem(me + n, 8)

    def tp_peer(n):
        return lax.rem(j + n, 8)

    barrier = pltpu.get_barrier_semaphore()
    for n in range(1, 8):
        pl.semaphore_signal(barrier, inc=1, device_id={"seq": seq_peer(n)}, device_id_type=MESH)
        pl.semaphore_signal(barrier, inc=1, device_id={"tp": tp_peer(n)}, device_id_type=MESH)
    for n in range(1, 4):
        device = {"grp": zh4 + lax.rem(y + n, 4)}
        pl.semaphore_signal(barrier, inc=1, device_id=device, device_id_type=MESH)
    pl.semaphore_signal(barrier, inc=1, device_id=dev_z, device_id_type=MESH)

    loads = {}
    for n, (name, src, dst) in enumerate(
        (
            ("cot", cot_in, cot_ref),
            ("proj_b", proj_b_in, proj_b.at[pl.ds(0, HB)]),
            ("fc", fc_b, fc_all.at[me, pl.ds(0, HB)]),
            ("head_b", head_b_in, head_b),
            ("mod_b", mod_b_in, mod_b),
            ("res_b", res_b_in, res_b),
            ("fcg", fc_g, fcg_all.at[me, pl.ds(0, HG)]),
            ("proj_g", proj_g_in, proj_g),
            ("head_g", head_g_in, head_g),
            ("mod_g", mod_g_in, mod_g),
            ("res_g", res_g_in, res_g),
        )
    ):
        loads[name] = pltpu.make_async_copy(src, dst, in_sem.at[n])
        loads[name].start()

    strength = table_ref[level_ref[0]]
    when = time_ref[0]
    pl.semaphore_wait(barrier, 18)

    def half(h):
        return pl.ds(h * (HB // 2), HB // 2)

    def hidden(s, h):
        return fc_all.at[s, half(h)]

    def seven(ref, send, recv):
        part = ref.at[pl.ds(0, 7)]
        return remote(part, part, send, recv, {"seq": sib})

    def hidden_copy(s, h, k, target, src=None):
        return remote(
            hidden(s, h) if src is None else src.at[half(h)], hidden(s, h), fc_send, fc_recv.at[s, h], {"seq": target}
        )

    to_r, to_l = 2 * xr + core, 2 * xl + core

    def go(copy):
        copy.start()

    def send_hidden(s, h, k, target, src=None):
        go(hidden_copy(s, h, k, target, src))

    def wait_hidden(s, h):
        hidden_copy(s, h, 0, sib).wait_recv()

    send_hidden(me, 0, 0, to_r, fc_b)
    send_hidden(me, 1, 1, to_l, fc_b)
    send_hidden(me, 0, 2, sib, fc_b)
    send_hidden(me, 1, 3, sib, fc_b)
    send_hidden(me, 1, 4, to_r, fc_b)
    send_hidden(me, 0, 5, to_l, fc_b)

    loads["cot"].wait()
    cot = cot_ref[...]
    cots[j] = (strength * cot).astype(BF16)
    for n in range(1, 8):
        go(remote(cots.at[j], cots.at[j], cot_send, cot_recv, {"tp": tp_peer(n)}))

    def pad_rows(value, rows):
        return jnp.concatenate([value, jnp.zeros((rows - value.shape[0], value.shape[1]), value.dtype)], axis=0)

    def pad_lanes(value, lanes):
        return jnp.concatenate([value, jnp.zeros((value.shape[0], lanes - value.shape[1]), value.dtype)], axis=1)

    for s in range(8):
        fc_all[s, HB:HBP, :] = jnp.zeros((HBP - HB, TOK), BF16)
        fcg_all[s, HG:HGP, :] = jnp.zeros((HGP - HG, TOK), BF16)
    proj_b[HB:HBP, :] = jnp.zeros((HBP - HB, WB), BF16)
    loads["mod_b"].wait()
    mods = pad_rows(
        jnp.concatenate([mod_b[n, pl.ds(when, 1), :] for n in range(3)], axis=0), 128
    )
    loads["res_b"].wait()
    for q in range(NC):
        turned = mods[:, 128 * q : 128 * q + 128].T
        at = slice(128 * q, 128 * q + 128)
        gate_b[at, :] = jnp.broadcast_to(turned[:, 0:1], (128, 128))
        shift_b[at, :] = jnp.broadcast_to(turned[:, 1:2], (128, 128))
        scale_b[at, :] = jnp.broadcast_to(1.0 + turned[:, 2:3], (128, 128))
        dev_b[at, :] = res_b[:, at].astype(F32).T
    mean = jnp.sum(dev_b[...], axis=0, keepdims=True) * (1.0 / WB)
    dev_b[...] -= mean
    means[j] = jnp.broadcast_to(mean, (8, TOK))
    for n in range(1, 8):
        go(remote(means.at[j], means.at[j], mn_send, mn_recv, {"tp": tp_peer(n)}))
    loads["proj_b"].wait()
    for q in range(NC):
        proj_bt[128 * q : 128 * q + 128, :] = proj_b[:, 128 * q : 128 * q + 128].T
    loads["fc"].wait()

    def terms(first, second):
        def one(i, carry):
            s = jnp.where(i == 0, first, second)
            term[s] = gate_b[...] * jnp.dot(proj_bt[...], fc_all[s], preferred_element_type=F32)

            @pl.when(s == j)
            def _():
                term[s] += dev_b[...]

            return carry

        lax.fori_loop(0, 2, one, 0)

    left, right, far = to_l, to_r, 2 * xf + core
    left_s, right_s, far_s = 2 * xl + 1 - core, 2 * xr + 1 - core, 2 * xf + 1 - core

    pairs = (
        x,
        1 - lax.rem(x, 2),
        jnp.where(x < 2, 2, x - 2),
        jnp.where(x == 3, 2, 3),
    )

    def block_at(b):
        n = lax.div(b, 2)
        pair = jnp.where(n == 0, pairs[0], jnp.where(n == 1, pairs[1], jnp.where(n == 2, pairs[2], pairs[3])))
        return 2 * pair + jnp.where(lax.rem(b, 2) == 0, core, 1 - core)

    def place_of(d):
        return sum(jnp.where(block_at(jnp.int32(b)) == d, b, 0) for b in range(8))

    wait_hidden(sib, 0)
    wait_hidden(sib, 1)
    terms(me, sib)

    def fcg_copy(s, n, target, src):
        return remote(src, fcg_all.at[s, pl.ds(0, HG)], fcg_send, fcg_recv.at[s], {"seq": target})

    relays = (
        (left, 0, 6, to_r),
        (left, 0, 7, sib),
        (right, 1, 8, to_l),
        (right, 1, 9, sib),
        (left, 1, 10, sib),
        (right, 0, 11, sib),
        (far, 0, 12, sib),
        (far, 1, 13, sib),
    )

    def relay(n):
        s, h, k, target = relays[n]
        hidden_copy(s, h, k, target).start()

    def scale_all():
        def one(d, carry):
            scaled_b[d] = (
                jnp.dot(head_bt[...], pad_rows(cots[d], 128), preferred_element_type=F32) * scale_b[...]
            )
            return carry

        lax.fori_loop(0, 8, one, 0)

    def near():
        wait_hidden(left, 0)
        relay(0)
        relay(1)
        wait_hidden(right, 1)
        relay(2)
        relay(3)
        wait_hidden(left, 1)
        relay(4)
        wait_hidden(right, 0)
        relay(5)
        for h in range(2):
            wait_hidden(left_s, h)
            wait_hidden(right_s, h)
        terms(2 * pairs[1], 2 * pairs[1] + 1)
        scale_all()

    def opposite():
        wait_hidden(far, 0)
        relay(6)
        wait_hidden(far, 1)
        relay(7)
        wait_hidden(far_s, 0)
        wait_hidden(far_s, 1)
        terms(2 * pairs[2], 2 * pairs[2] + 1)
        for n in range(1, 8):
            fcg_copy(me, n, seq_peer(n), fc_g).start()

    def rest():
        terms(2 * pairs[3], 2 * pairs[3] + 1)

    in_left = j < 4
    place = jnp.where(in_left, j, 7 - j)
    toward = {"tp": jnp.where(in_left, j + 1, j - 1)}
    away = {"tp": jnp.where(in_left, j - 1, j + 1)}

    def piece(q):
        return pl.ds(pl.multiple_of(q * SUB, 16), SUB)

    def in_copy(b, q):
        return remote(put.at[b, piece(q)], got.at[b, piece(q)], in_send, in_recv.at[b, q], toward)

    def cross_copy(b, q):
        return remote(put.at[b, piece(q)], cross.at[b, piece(q)], in_send, cross_recv.at[b, q], toward)

    def out_copy(b, q):
        ref = spread.at[b, piece(q)]
        return remote(ref, ref, out_send, out_recv.at[b, q], away)

    def stat_copy(s, n, d, target):
        ref = stats.at[d, s]
        return remote(ref, ref, st_send, st_recv.at[d], {"seq": target})

    def block_stats(d, b):
        up = scaled_b[d]
        value = spread[b].astype(F32)
        mean = jnp.sum(value, axis=0, keepdims=True) * (1.0 / WB)
        value -= mean
        stats[d, me] = pad_rows(
            jnp.concatenate(
                [
                    means[d, 0:1] + mean,
                    jnp.sum(value * value, axis=0, keepdims=True),
                    jnp.sum(up, axis=0, keepdims=True),
                    jnp.sum(up * value, axis=0, keepdims=True),
                ],
                axis=0,
            ),
            8,
        )
        for n in range(1, 8):
            stat_copy(me, n, d, seq_peer(n)).start()

    def norm(every, mine, width, whole):
        centre = sum(r[0:1] for r in every) * (1.0 / 8)
        gaps = [r[0:1] - centre for r in every]
        square_sum = sum(r[1:2] + width * (g * g) for r, g in zip(every, gaps))
        inverse = lax.rsqrt(square_sum * (1.0 / whole) + EPSILON)
        first = sum(r[2:3] for r in every) * (1.0 / whole)
        cross_sum = sum(r[3:4] + r[2:3] * g for r, g in zip(every, gaps))
        second = inverse * cross_sum * (1.0 / whole)
        offset = inverse * (mine - centre)
        return inverse, offset, inverse * inverse * second, inverse * (first + offset * second)

    def consume(d):
        d = jnp.int32(d)
        b = place_of(d)
        seven(stats.at[d], st_send, st_recv.at[d]).wait_recv()
        every = [stats[d, s] for s in range(8)]
        inverse, offset, slope, base = norm(every, means[d, 0:1], float(WB), float(DB))
        facts[d] = pad_rows(jnp.concatenate([inverse, offset, slope, base], axis=0), 8)
        value = spread[b].astype(F32)
        signal[d] = (
            gate_b[...] * (inverse * scaled_b[d] - slope * value - base)
        ).astype(BF16)
        shaped = ((inverse * value + offset) * scale_b[...] + shift_b[...]).astype(BF16)
        head_sum[...] += lax.dot_general(
            cots[d], shaped, (((1,), (1,)), ((), ())), preferred_element_type=F32
        )

    def guide_copy(right_way, i):
        if right_way:
            return remote(putg_r.at[i], gotg_r.at[i], rg_send.at[i], rg_recv.at[i], {"tp": j + 1})
        return remote(putg_l.at[i], gotg_l.at[i], lg_send.at[i], lg_recv.at[i], {"tp": j - 1})

    def guide_term(s):
        @pl.when(s != me)
        def _():
            fcg_copy(s, 0, s, fcg_all.at[s, pl.ds(0, HG)]).wait_recv()

        return jnp.dot(proj_gp[...], fcg_all[s], preferred_element_type=F32)

    def guide_step(t):
        for right_way in (True, False):
            far_end = j if right_way else 7 - j
            w = t - UNITS - SKEW * far_end
            i = lax.div(w, GSTEP)
            put, got = (putg_r, gotg_r) if right_way else (putg_l, gotg_l)

            @pl.when((w >= 0) & (lax.rem(w, GSTEP) == 0) & (i < 7 - far_end))
            def _():
                own = guide_term(7 - i if right_way else i)

                @pl.when(far_end > 0)
                def _():
                    guide_copy(right_way, i).wait_recv()
                    put[i] = (got[i].astype(F32) + own).astype(BF16)

                @pl.when(far_end == 0)
                def _():
                    put[i] = own.astype(BF16)

                guide_copy(right_way, i).start()

    def tick(t, carry):
        for at, action in ((2, near), (4, opposite), (6, rest)):
            pl.when(t == at * NQ)(action)
        u = t - SKEW * place

        @pl.when((u >= 0) & (u < UNITS))
        def _():
            b = lax.div(u, NQ)
            q = lax.rem(u, NQ)
            own = term[block_at(b), piece(q), :]

            @pl.when(place > 0)
            def _():
                in_copy(b, q).wait_recv()
                put[b, piece(q), :] = (got[b, piece(q), :].astype(F32) + own).astype(BF16)

            @pl.when(place == 0)
            def _():
                put[b, piece(q), :] = own.astype(BF16)

            @pl.when(place < 3)
            def _():
                in_copy(b, q).start()

            @pl.when(place == 3)
            def _():
                cross_copy(b, q).start()

        v = t - SKEW * (7 - place)

        @pl.when((v >= 0) & (v < UNITS))
        def _():
            b = lax.div(v, NQ)
            q = lax.rem(v, NQ)

            @pl.when(place == 3)
            def _():
                cross_copy(b, q).wait_recv()
                spread[b, piece(q), :] = add(put[b, piece(q), :], cross[b, piece(q), :])

            @pl.when(place < 3)
            def _():
                out_copy(b, q).wait_recv()

            @pl.when(place > 0)
            def _():
                out_copy(b, q).start()

            for d, (at_b, at_q) in enumerate(((6, 3), (7, 0), (7, 1), (7, 2))):

                @pl.when((b == at_b) & (q == at_q))
                def _():
                    consume(d)

            @pl.when(q == NQ - 1)
            def _():
                block_stats(block_at(b), b)

        guide_step(t)
        return carry

    def add(a, b):
        return (a.astype(F32) + b.astype(F32)).astype(BF16)

    loads["head_b"].wait()
    head_bt[...] = pad_lanes(head_b[...].T, 128)
    loads["proj_g"].wait()
    proj_gp[...] = pad_lanes(proj_g[...], HGP)
    loads["fcg"].wait()
    head_sum[...] = jnp.zeros_like(head_sum)
    seven(cots, cot_send, cot_recv).wait_recv()
    seven(means, mn_send, mn_recv).wait_recv()

    lax.fori_loop(0, UNITS + 7 * SKEW, tick, 0)
    for d in range(4, 8):
        consume(d)

    def rows(shard):
        return pl.ds(pl.multiple_of(shard * SHARD, 16), SHARD)

    def y_peer(n):
        return lax.rem(y + n, 4)

    def one_copy(c, n):
        p = y_peer(n)
        return remote(grad.at[c, rows(p)], ones.at[c, n - 1], one_send, one_recv.at[c], {"grp": zh4 + p})

    def z_copy(c):
        return remote(zed.at[c], zed_in.at[c], z_send, z_recv.at[c], dev_z)

    def back_copy(c, n):
        ref = final.at[c, rows(y)]
        return remote(ref, ref, g1_send, g1_recv.at[c], {"grp": zh4 + y_peer(n)})

    def three(c, send, recv):
        part = final.at[c, pl.ds(0, 3 * SHARD)]
        return remote(part, part, send, recv, dev_z)

    patch_rows = head_sum[pl.ds(pl.multiple_of(j * 8, 8), 8), :]
    spare = [patch_rows[:, 128 * q : 128 * q + 128] for q in range(NC)]
    spare = [
        jnp.concatenate(spare[0:4], axis=0),
        pad_rows(spare[4], 32),
    ] + [jnp.zeros((32, 128), F32)] * 3
    def guide_stats():
        loads["head_g"].wait()
        loads["mod_g"].wait()
        loads["res_g"].wait()
        mods = jnp.concatenate([mod_g[n, pl.ds(when, 1), :] for n in range(3)], axis=0)
        mods = pad_rows(pad_lanes(mods, 256), 128)
        for q in range(2):
            high = min(128, WG - 128 * q)
            turned = mods[:, 128 * q : 128 * q + 128].T[0:high]
            at = slice(128 * q, 128 * q + high)
            gate_g[at, :] = jnp.broadcast_to(turned[:, 0:1], (high, 128))
            shift_g[at, :] = jnp.broadcast_to(turned[:, 1:2], (high, 128))
            scale_g[at, :] = jnp.broadcast_to(1.0 + turned[:, 2:3], (high, 128))
        cot_g = ((1.0 - strength) * cot_ref[...]).astype(BF16)
        scaled_g[...] = (
            lax.dot_general(head_g[...], cot_g, (((0,), (0,)), ((), ())), preferred_element_type=F32)
            * scale_g[...]
        )
        term_g[...] = guide_term(j)
        for right_way in (True, False):
            place = j if right_way else 7 - j
            got = gotg_r if right_way else gotg_l

            @pl.when(place > 0)
            def _():
                guide_copy(right_way, 7 - place).wait_recv()
                term_g[...] += got[7 - place].astype(F32)

        stream = res_g[...].astype(F32) + gate_g[...] * term_g[...]
        mean_g = jnp.sum(stream, axis=0, keepdims=True) * (1.0 / WG)
        away_g = stream - mean_g
        dev_g[...] = away_g
        up_g = scaled_g[...]
        stats_g[me] = pad_rows(
            jnp.concatenate(
                [
                    mean_g,
                    jnp.sum(away_g * away_g, axis=0, keepdims=True),
                    jnp.sum(up_g, axis=0, keepdims=True),
                    jnp.sum(up_g * away_g, axis=0, keepdims=True),
                ],
                axis=0,
            ),
            8,
        )
        for n in range(1, 8):
            go(remote(stats_g.at[me], stats_g.at[me], sg_send, sg_recv, {"seq": seq_peer(n)}))

    own_at = place_of(j)

    def own_big():
        inverse, offset, slope, base = (facts[j, n : n + 1, :] for n in range(4))
        value = spread[own_at].astype(F32)
        own = inverse * scaled_b[j] - slope * value - base
        for q in range(NC):
            grad_res_b[:, 128 * q : 128 * q + 128] = own[128 * q : 128 * q + 128, :].T.astype(BF16)
        shaped = ((inverse * value + offset) * scale_b[...] + shift_b[...]).astype(BF16)
        made_b[...] = strength * jnp.dot(head_b[...], shaped, preferred_element_type=F32)
    def own_guide():
        seven(stats_g, sg_send, sg_recv).wait_recv()
        inverse, offset, slope, base = norm([stats_g[s] for s in range(8)], stats_g[me][0:1], float(WG), float(DG))
        grad_res_g[...] = (inverse * scaled_g[...] - slope * dev_g[...] - base).astype(BF16)
        shaped = ((inverse * dev_g[...] + offset) * scale_g[...] + shift_g[...]).astype(BF16)
        out_g = jnp.dot(head_g[...], shaped, preferred_element_type=F32)
        parts[me] = (made_b[...] + (1.0 - strength) * out_g).astype(BF16)
        for n in range(1, 8):
            go(remote(parts.at[me], parts.at[me], pt_send, pt_recv, {"seq": seq_peer(n)}))

    def settle():
        part = fc_all.at[pl.ds(0, 7), pl.ds(0, HB)]
        remote(part, part, fc_send, fc_recv.at[0, 0], {"seq": sib}).wait_send()
        part = fcg_all.at[pl.ds(0, 7), pl.ds(0, HG)]
        remote(part, part, fcg_send, fcg_recv.at[0], {"seq": sib}).wait_send()
        seven(cots, cot_send, cot_recv).wait_send()
        seven(means, mn_send, mn_recv).wait_send()
        remote(put, got, in_send, in_recv.at[0, 0], {"seq": sib}).wait_send()

        @pl.when(place > 0)
        def _():
            remote(spread, spread, out_send, out_recv.at[0, 0], {"seq": sib}).wait_send()

        part = scaled_b.at[0, pl.ds(0, 7 * 8 * 8)]
        remote(part, part, st_send, st_recv.at[0], {"seq": sib}).wait_send()

        def drain(b, carry):
            for right_way in (True, False):

                @pl.when(b < (7 - j if right_way else j))
                def _():
                    guide_copy(right_way, b).wait_send()

            return carry

        lax.fori_loop(0, 7, drain, 0)

    def stage_grad(c):
        at = slice(128 * c, 128 * c + 128)
        grad[c, 0:HB, :] = lax.dot_general(
            jnp.concatenate([fc_all[s, 0:HB, :] for s in range(8)], axis=1),
            jnp.concatenate([signal[s, at, :] for s in range(8)], axis=1),
            (((1,), (1,)), ((), ())),
            preferred_element_type=F32,
        ).astype(BF16)
        grad[c, HB:HBP, :] = spare[c].astype(BF16)
        for n in (1, 3, 2):
            go(one_copy(c, n))

    def stage_one(c):
        three(c, one_send, one_recv.at[c]).wait_recv()
        total = grad[c, rows(y), :].astype(F32)
        for n in range(3):
            total += ones[c, n].astype(F32)
        zed[c] = total.astype(BF16)
        go(z_copy(c))

    def stage_z(c):
        z_copy(c).wait_recv()
        final[c, rows(y), :] = add(zed[c], zed_in[c])
        for n in (2, 1, 3):
            go(back_copy(c, n))

    def stage_out(c):
        three(c, g1_send, g1_recv.at[c]).wait_recv()
        grad_proj_ref[:, 128 * c : 128 * c + 128] = final[c, 0:HB, :]
        if c == 1:
            heads[j, 0:32, :] = final[0, HB:HBP, :]
            heads[j, 32:64, :] = final[1, HB:HBP, :]
            for n in range(1, 8):
                go(remote(heads.at[j], heads.at[j], hd_send, hd_recv, {"tp": tp_peer(n)}))

    def predict():
        seven(parts, pt_send, pt_recv).wait_recv()
        guided_ref[...] = sum(parts[s].astype(F32) for s in range(8))

    def collect_heads():
        seven(heads, hd_send, hd_recv).wait_recv()
        for p in range(8):
            block = heads[p].astype(F32)
            for q in range(NC):
                grad_head_ref[8 * p : 8 * p + 8, 128 * q : 128 * q + 128] = block[8 * q : 8 * q + 8]

    A, B, C, D = stage_grad, stage_one, stage_z, stage_out
    for stage, c in ((A, 0), (A, 1), (B, 0), (A, 2), (B, 1), (A, 3), (A, 4), (B, 2), (B, 3)):
        stage(c)
    guide_stats()
    for stage, c in ((B, 4), (C, 0)):
        stage(c)
    own_big()
    own_guide()
    C(1)
    D(0)
    settle()
    C(2)
    D(1)
    predict()
    C(3)
    D(2)
    collect_heads()
    C(4)
    D(3)
    D(4)

    whole = final.at[:, pl.ds(0, 3 * SHARD)]
    remote(whole, whole, one_send, one_recv.at[0], dev_z).wait_send()
    remote(zed, zed_in, z_send, z_recv.at[0], dev_z).wait_send()
    remote(whole, whole, g1_send, g1_recv.at[0], dev_z).wait_send()
    seven(stats_g, sg_send, sg_recv).wait_send()
    seven(parts, pt_send, pt_recv).wait_send()
    seven(heads, hd_send, hd_recv).wait_send()


def shards(
    fc_big,
    fc_guide,
    res_big,
    res_guide,
    cotangent,
    proj_big,
    proj_guide,
    head_big,
    head_guide,
    modulation_big,
    modulation_guide,
    weight_table,
    time_index,
    weight_index,
):
    smem = pl.BlockSpec(memory_space=pltpu.SMEM)
    vmem = pl.BlockSpec(memory_space=pltpu.VMEM)
    hbm = pl.BlockSpec(memory_space=pl.ANY)
    dma = pltpu.SemaphoreType.DMA
    V = pltpu.VMEM
    shapes = (
        ((PATCH, TOK), F32),
        ((HB, WB), BF16),
        ((PATCH, WB), F32),
        ((TOK, WB), BF16),
        ((WG, TOK), BF16),
    )
    made = pl.pallas_call(
        kernel,
        out_shape=tuple(V(*s) for s in shapes),
        in_specs=[smem] * 3 + [hbm] * 11,
        out_specs=(vmem,) * 5,
        scratch_shapes=[
            V((TOK, WB), BF16),
            V((WG, TOK), BF16),
            V((PATCH, TOK), F32),
            V((HBP, WB), BF16),
            V((WG, HG), BF16),
            V((PATCH, WB), BF16),
            V((PATCH, WG), BF16),
            V((3, STEPS, WB), F32),
            V((3, STEPS, WG), F32),
            V((WB, HBP), BF16),
            V((WG, HGP), BF16),
            V((WB, 128), BF16),
            V((WB, 128), F32),
            V((WB, 128), F32),
            V((WB, 128), F32),
            V((WG, 128), F32),
            V((WG, 128), F32),
            V((WG, 128), F32),
            V((8, HBP, TOK), BF16),
            V((8, HGP, TOK), BF16),
            V((8, WB, TOK), F32),
            V((WG, TOK), F32),
            V((8, WB, TOK), BF16),
            V((8, WB, TOK), BF16),
            V((8, WB, TOK), BF16),
            V((8, 8, TOK), F32),
            V((7, WG, TOK), BF16),
            V((7, WG, TOK), BF16),
            V((7, WG, TOK), BF16),
            V((7, WG, TOK), BF16),
            V((WB, TOK), F32),
            V((WG, TOK), F32),
            V((8, WB, TOK), F32),
            V((WG, TOK), F32),
            V((8, WB, TOK), BF16),
            V((8, PATCH, TOK), BF16),
            V((8, 8, 8, TOK), F32),
            V((8, 8, TOK), F32),
            V((8, 8, TOK), F32),
            V((8, WB, TOK), BF16),
            V((PATCH, WB), F32),
            V((8, PATCH, TOK), BF16),
            V((NC, HBP, 128), BF16),
            V((NC, 3, SHARD, 128), BF16),
            V((NC, SHARD, 128), BF16),
            V((NC, SHARD, 128), BF16),
            V((NC, HBP, 128), BF16),
            V((8, 64, 128), BF16),
            V((PATCH, TOK), F32),
            dma((11,)),
            dma(()),
            dma((8, 2)),
            dma(()),
            dma((8,)),
            dma(()),
            dma(()),
            dma(()),
            dma(()),
            dma(()),
            dma((8, NQ)),
            dma((8, NQ)),
            dma(()),
            dma((8, NQ)),
            dma((7,)),
            dma((7,)),
            dma((7,)),
            dma((7,)),
            dma(()),
            dma((8,)),
            dma(()),
            dma(()),
            dma(()),
            dma(()),
            dma(()),
            dma((NC,)),
            dma(()),
            dma((NC,)),
            dma(()),
            dma((NC,)),
            dma(()),
            dma(()),
        ],
        compiler_params=pltpu.CompilerParams(
            collective_id=0, has_side_effects=True, vmem_limit_bytes=56 * 2**20
        ),
    )(
        time_index,
        weight_index,
        weight_table,
        fc_big.T,
        fc_guide.T,
        res_big,
        res_guide.T,
        cotangent.T,
        proj_big,
        proj_guide.T,
        head_big.T,
        head_guide.T,
        modulation_big.transpose(1, 0, 2),
        modulation_guide.transpose(1, 0, 2),
    )
    guided, grad_proj, grad_head, grad_res_big, grad_res_guide = made
    return guided.T, grad_proj, grad_head.T, grad_res_big, grad_res_guide.T


def solution(mesh):
    placed = (
        P(("grp", "seq"), "tp"),
        P(("grp", "seq"), "tp"),
        P(("grp", "tp"), "seq"),
        P(("grp", "tp"), "seq"),
        P(("grp", "tp"), None),
        P("tp", "seq"),
        P("tp", "seq"),
        P("seq", None),
        P("seq", None),
        P(None, None, "seq"),
        P(None, None, "seq"),
        P(),
        P("grp"),
        P("grp"),
    )
    return jax.shard_map(
        shards,
        mesh=mesh,
        in_specs=placed,
        out_specs=(
            P(("grp", "tp"), None),
            P("tp", "seq"),
            P("seq", None),
            P(("grp", "tp"), "seq"),
            P(("grp", "tp"), "seq"),
        ),
        check_vma=False,
    )
```

```python
import jax
import jax.numpy as jnp
from jax import lax
from jax.experimental import pallas as pl
from jax.experimental.pallas import tpu as pltpu
from jax.sharding import PartitionSpec as P

MESH = pl.DeviceIdType.MESH
F32 = jnp.float32
BF16 = jnp.bfloat16

DB = 5120
DG = 1536
EPSILON = 1e-06

TOK = 128
WB = 640
WG = 192
HB = 864
HBP = 896
HG = 560
HGP = 640
PATCH = 64
STEPS = 50
NQ = 5
SUB = WB // NQ
UNITS = 8 * NQ
SKEW = 6
DEPTH = 3
GSTEP = 2
NC = 5
SHARD = 224


def remote(src, dst, send, recv, device):
    return pltpu.make_async_remote_copy(
        src_ref=src, dst_ref=dst, send_sem=send, recv_sem=recv, device_id=device, device_id_type=MESH
    )


def kernel(
    time_ref,
    level_ref,
    table_ref,
    fc_b,
    fc_g,
    res_b_in,
    res_g_in,
    cot_in,
    proj_b_in,
    proj_g_in,
    head_b_in,
    head_g_in,
    mod_b_in,
    mod_g_in,
    guided_ref,
    grad_proj_ref,
    grad_head_ref,
    grad_res_b,
    grad_res_g,
    res_b,
    res_g,
    cot_ref,
    proj_b,
    proj_g,
    head_b,
    head_g,
    mod_b,
    mod_g,
    proj_bt,
    proj_gp,
    head_bt,
    gate_b,
    shift_b,
    scale_b,
    gate_g,
    shift_g,
    scale_g,
    fc_all,
    fcg_all,
    term,
    term_g,
    got,
    put,
    cross,
    means,
    gotg_r,
    gotg_l,
    putg_r,
    putg_l,
    dev_b,
    dev_g,
    scaled_b,
    scaled_g,
    spread,
    cots,
    stats,
    stats_g,
    facts,
    signal,
    head_sum,
    parts,
    grad,
    ones,
    zed,
    zed_in,
    final,
    heads,
    made_b,
    in_sem,
    fc_send,
    fc_recv,
    fcg_send,
    fcg_recv,
    cot_send,
    cot_recv,
    mn_send,
    mn_recv,
    in_send,
    in_recv,
    out_send,
    out_recv,
    rg_send,
    rg_recv,
    lg_send,
    lg_recv,
    st_send,
    st_recv,
    sg_send,
    sg_recv,
    pt_send,
    pt_recv,
    one_send,
    one_recv,
    z_send,
    z_recv,
    g1_send,
    g1_recv,
    hd_send,
    hd_recv,
):
    grp = lax.axis_index("grp")
    me = lax.axis_index("seq")
    j = lax.axis_index("tp")
    y = lax.rem(grp, 4)
    zh4 = grp - y
    x = lax.div(me, 2)
    core = lax.rem(me, 2)
    sib = me + 1 - 2 * core
    xr = lax.rem(x + 1, 4)
    xl = lax.rem(x + 3, 4)
    xf = lax.rem(x + 2, 4)
    dev_z = {"grp": lax.rem(grp + 4, 8)}

    def seq_peer(n):
        return lax.rem(me + n, 8)

    def tp_peer(n):
        return lax.rem(j + n, 8)

    barrier = pltpu.get_barrier_semaphore()
    for n in range(1, 8):
        pl.semaphore_signal(barrier, inc=1, device_id={"seq": seq_peer(n)}, device_id_type=MESH)
        pl.semaphore_signal(barrier, inc=1, device_id={"tp": tp_peer(n)}, device_id_type=MESH)
    for n in range(1, 4):
        device = {"grp": zh4 + lax.rem(y + n, 4)}
        pl.semaphore_signal(barrier, inc=1, device_id=device, device_id_type=MESH)
    pl.semaphore_signal(barrier, inc=1, device_id=dev_z, device_id_type=MESH)

    loads = {}
    for n, (name, src, dst) in enumerate(
        (
            ("cot", cot_in, cot_ref),
            ("proj_b", proj_b_in, proj_b.at[pl.ds(0, HB)]),
            ("fc", fc_b, fc_all.at[me, pl.ds(0, HB)]),
            ("head_b", head_b_in, head_b),
            ("mod_b", mod_b_in, mod_b),
            ("res_b", res_b_in, res_b),
            ("fcg", fc_g, fcg_all.at[me, pl.ds(0, HG)]),
            ("proj_g", proj_g_in, proj_g),
            ("head_g", head_g_in, head_g),
            ("mod_g", mod_g_in, mod_g),
            ("res_g", res_g_in, res_g),
        )
    ):
        loads[name] = pltpu.make_async_copy(src, dst, in_sem.at[n])
        loads[name].start()

    strength = table_ref[level_ref[0]]
    when = time_ref[0]
    pl.semaphore_wait(barrier, 18)

    def half(h):
        return pl.ds(h * (HB // 2), HB // 2)

    def hidden(s, h):
        return fc_all.at[s, half(h)]

    def seven(ref, send, recv):
        part = ref.at[pl.ds(0, 7)]
        return remote(part, part, send, recv, {"seq": sib})

    def hidden_copy(s, h, k, target, src=None):
        return remote(
            hidden(s, h) if src is None else src.at[half(h)], hidden(s, h), fc_send, fc_recv.at[s, h], {"seq": target}
        )

    to_r, to_l = 2 * xr + core, 2 * xl + core

    def go(copy):
        copy.start()

    def send_hidden(s, h, k, target, src=None):
        go(hidden_copy(s, h, k, target, src))

    def wait_hidden(s, h):
        hidden_copy(s, h, 0, sib).wait_recv()

    send_hidden(me, 0, 0, to_r, fc_b)
    send_hidden(me, 1, 1, to_l, fc_b)
    send_hidden(me, 0, 2, sib, fc_b)
    send_hidden(me, 1, 3, sib, fc_b)
    send_hidden(me, 1, 4, to_r, fc_b)
    send_hidden(me, 0, 5, to_l, fc_b)

    loads["cot"].wait()
    cot = cot_ref[...]
    cots[j] = (strength * cot).astype(BF16)
    for n in range(1, 8):
        go(remote(cots.at[j], cots.at[j], cot_send, cot_recv, {"tp": tp_peer(n)}))

    def pad_rows(value, rows):
        return jnp.concatenate([value, jnp.zeros((rows - value.shape[0], value.shape[1]), value.dtype)], axis=0)

    def pad_lanes(value, lanes):
        return jnp.concatenate([value, jnp.zeros((value.shape[0], lanes - value.shape[1]), value.dtype)], axis=1)

    for s in range(8):
        fc_all[s, HB:HBP, :] = jnp.zeros((HBP - HB, TOK), BF16)
        fcg_all[s, HG:HGP, :] = jnp.zeros((HGP - HG, TOK), BF16)
    proj_b[HB:HBP, :] = jnp.zeros((HBP - HB, WB), BF16)
    loads["mod_b"].wait()
    mods = pad_rows(
        jnp.concatenate([mod_b[n, pl.ds(when, 1), :] for n in range(3)], axis=0), 128
    )
    loads["res_b"].wait()
    for q in range(NC):
        turned = mods[:, 128 * q : 128 * q + 128].T
        at = slice(128 * q, 128 * q + 128)
        gate_b[at, :] = jnp.broadcast_to(turned[:, 0:1], (128, 128))
        shift_b[at, :] = jnp.broadcast_to(turned[:, 1:2], (128, 128))
        scale_b[at, :] = jnp.broadcast_to(1.0 + turned[:, 2:3], (128, 128))
        dev_b[at, :] = res_b[:, at].astype(F32).T
    mean = jnp.sum(dev_b[...], axis=0, keepdims=True) * (1.0 / WB)
    dev_b[...] -= mean
    means[j] = jnp.broadcast_to(mean, (8, TOK))
    for n in range(1, 8):
        go(remote(means.at[j], means.at[j], mn_send, mn_recv, {"tp": tp_peer(n)}))
    loads["proj_b"].wait()
    for q in range(NC):
        proj_bt[128 * q : 128 * q + 128, :] = proj_b[:, 128 * q : 128 * q + 128].T
    loads["fc"].wait()

    def terms(s):
        term[s] = gate_b[...] * jnp.dot(proj_bt[...], fc_all[s], preferred_element_type=F32)

        @pl.when(s == j)
        def _():
            term[s] += dev_b[...]

    left, right, far = to_l, to_r, 2 * xf + core
    left_s, right_s, far_s = 2 * xl + 1 - core, 2 * xr + 1 - core, 2 * xf + 1 - core

    pairs = (
        x,
        1 - lax.rem(x, 2),
        jnp.where(x < 2, 2, x - 2),
        jnp.where(x == 3, 2, 3),
    )

    def block_at(b):
        n = lax.div(b, 2)
        pair = jnp.where(n == 0, pairs[0], jnp.where(n == 1, pairs[1], jnp.where(n == 2, pairs[2], pairs[3])))
        return 2 * pair + jnp.where(lax.rem(b, 2) == 0, core, 1 - core)

    def place_of(d):
        return sum(jnp.where(block_at(jnp.int32(b)) == d, b, 0) for b in range(8))

    terms(me)

    def fcg_copy(s, n, target, src):
        return remote(src, fcg_all.at[s, pl.ds(0, HG)], fcg_send, fcg_recv.at[s], {"seq": target})

    relays = (
        (left, 0, 6, to_r),
        (left, 0, 7, sib),
        (right, 1, 8, to_l),
        (right, 1, 9, sib),
        (left, 1, 10, sib),
        (right, 0, 11, sib),
        (far, 0, 12, sib),
        (far, 1, 13, sib),
    )

    def relay(n):
        s, h, k, target = relays[n]
        hidden_copy(s, h, k, target).start()

    def scale_all():
        def one(d, carry):
            scaled_b[d] = (
                jnp.dot(head_bt[...], pad_rows(cots[d], 128), preferred_element_type=F32) * scale_b[...]
            )
            return carry

        lax.fori_loop(0, 8, one, 0)

    def beside():
        wait_hidden(sib, 0)
        wait_hidden(sib, 1)

    def near():
        wait_hidden(left, 0)
        relay(0)
        relay(1)
        wait_hidden(right, 1)
        relay(2)
        relay(3)

    def near_rest():
        wait_hidden(left, 1)
        relay(4)
        wait_hidden(right, 0)
        relay(5)

    def near_others():
        for h in range(2):
            wait_hidden(left_s, h)
            wait_hidden(right_s, h)

    def opposite():
        wait_hidden(far, 0)
        relay(6)
        wait_hidden(far, 1)
        relay(7)

    def opposite_others():
        wait_hidden(far_s, 0)
        wait_hidden(far_s, 1)
        for n in range(1, 8):
            fcg_copy(me, n, seq_peer(n), fc_g).start()

    events = (
        (NQ, beside),
        (2 * NQ - 2, near),
        (2 * NQ, near_rest),
        (2 * NQ + 2, scale_all),
        (3 * NQ, near_others),
        (4 * NQ - 2, opposite),
        (5 * NQ, opposite_others),
    )

    in_left = j < 4
    place = jnp.where(in_left, j, 7 - j)
    toward = {"tp": jnp.where(in_left, j + 1, j - 1)}
    away = {"tp": jnp.where(in_left, j - 1, j + 1)}

    def piece(q):
        return pl.ds(pl.multiple_of(q * SUB, 16), SUB)

    def in_copy(b, q):
        return remote(put.at[b, piece(q)], got.at[b, piece(q)], in_send.at[lax.rem(b * NQ + q, DEPTH)], in_recv.at[b, q], toward)

    def cross_copy(b, q):
        return remote(put.at[b, piece(q)], cross.at[b, piece(q)], in_send.at[lax.rem(b * NQ + q, DEPTH)], out_recv.at[b, q], toward)

    def out_copy(b, q):
        ref = spread.at[b, piece(q)]
        return remote(ref, ref, out_send, out_recv.at[b, q], away)

    def stat_copy(s, n, d, target):
        ref = stats.at[d, s]
        return remote(ref, ref, st_send, st_recv.at[d], {"seq": target})

    def block_stats(d, b):
        up = scaled_b[d]
        value = spread[b].astype(F32)
        mean = jnp.sum(value, axis=0, keepdims=True) * (1.0 / WB)
        value -= mean
        stats[d, me] = pad_rows(
            jnp.concatenate(
                [
                    means[d, 0:1] + mean,
                    jnp.sum(value * value, axis=0, keepdims=True),
                    jnp.sum(up, axis=0, keepdims=True),
                    jnp.sum(up * value, axis=0, keepdims=True),
                ],
                axis=0,
            ),
            8,
        )
        for n in range(1, 8):
            stat_copy(me, n, d, seq_peer(n)).start()

    def norm(every, mine, width, whole):
        centre = sum(r[0:1] for r in every) * (1.0 / 8)
        gaps = [r[0:1] - centre for r in every]
        square_sum = sum(r[1:2] + width * (g * g) for r, g in zip(every, gaps))
        inverse = lax.rsqrt(square_sum * (1.0 / whole) + EPSILON)
        first = sum(r[2:3] for r in every) * (1.0 / whole)
        cross_sum = sum(r[3:4] + r[2:3] * g for r, g in zip(every, gaps))
        second = inverse * cross_sum * (1.0 / whole)
        offset = inverse * (mine - centre)
        return inverse, offset, inverse * inverse * second, inverse * (first + offset * second)

    def consume(d):
        d = jnp.int32(d)
        b = place_of(d)
        seven(stats.at[d], st_send, st_recv.at[d]).wait_recv()
        every = [stats[d, s] for s in range(8)]
        inverse, offset, slope, base = norm(every, means[d, 0:1], float(WB), float(DB))
        facts[d] = pad_rows(jnp.concatenate([inverse, offset, slope, base], axis=0), 8)
        value = spread[b].astype(F32)
        signal[d] = (
            gate_b[...] * (inverse * scaled_b[d] - slope * value - base)
        ).astype(BF16)
        shaped = ((inverse * value + offset) * scale_b[...] + shift_b[...]).astype(BF16)
        head_sum[...] += lax.dot_general(
            cots[d], shaped, (((1,), (1,)), ((), ())), preferred_element_type=F32
        )

    def guide_copy(right_way, i):
        if right_way:
            return remote(putg_r.at[i], gotg_r.at[i], rg_send.at[i], rg_recv.at[i], {"tp": j + 1})
        return remote(putg_l.at[i], gotg_l.at[i], lg_send.at[i], lg_recv.at[i], {"tp": j - 1})

    def guide_term(s):
        @pl.when(s != me)
        def _():
            fcg_copy(s, 0, s, fcg_all.at[s, pl.ds(0, HG)]).wait_recv()

        return jnp.dot(proj_gp[...], fcg_all[s], preferred_element_type=F32)

    def guide_step(t):
        for right_way in (True, False):
            far_end = j if right_way else 7 - j
            w = t - UNITS - SKEW * far_end
            i = lax.div(w, GSTEP)
            put, got = (putg_r, gotg_r) if right_way else (putg_l, gotg_l)

            @pl.when((w >= 0) & (lax.rem(w, GSTEP) == 0) & (i < 7 - far_end))
            def _():
                own = guide_term(7 - i if right_way else i)

                @pl.when(far_end > 0)
                def _():
                    guide_copy(right_way, i).wait_recv()
                    put[i] = (got[i].astype(F32) + own).astype(BF16)

                @pl.when(far_end == 0)
                def _():
                    put[i] = own.astype(BF16)

                guide_copy(right_way, i).start()

    def tick(t, carry):
        for at, action in events:
            pl.when(t == at)(action)

        @pl.when((lax.rem(t, NQ) == 0) & (t > 0) & (t < UNITS))
        def _():
            terms(block_at(lax.div(t, NQ)))

        u = t - SKEW * place

        @pl.when((u >= 0) & (u < UNITS))
        def _():
            b = lax.div(u, NQ)
            q = lax.rem(u, NQ)
            own = term[block_at(b), piece(q), :]

            @pl.when(place > 0)
            def _():
                in_copy(b, q).wait_recv()
                put[b, piece(q), :] = (got[b, piece(q), :].astype(F32) + own).astype(BF16)

            @pl.when(place == 0)
            def _():
                put[b, piece(q), :] = own.astype(BF16)

            @pl.when(u >= DEPTH)
            def _():
                in_copy(b, q).wait_send()

            @pl.when(place < 3)
            def _():
                in_copy(b, q).start()

            @pl.when(place == 3)
            def _():
                cross_copy(b, q).start()

        v = t - SKEW * (7 - place)

        @pl.when((v >= 0) & (v < UNITS))
        def _():
            b = lax.div(v, NQ)
            q = lax.rem(v, NQ)

            @pl.when(place == 3)
            def _():
                cross_copy(b, q).wait_recv()
                spread[b, piece(q), :] = add(put[b, piece(q), :], cross[b, piece(q), :])

            @pl.when(place < 3)
            def _():
                out_copy(b, q).wait_recv()

            @pl.when(place > 0)
            def _():
                out_copy(b, q).start()

            for d, (at_b, at_q) in enumerate(((6, 3), (7, 0), (7, 1), (7, 2))):

                @pl.when((b == at_b) & (q == at_q))
                def _():
                    consume(d)

            @pl.when(q == NQ - 1)
            def _():
                block_stats(block_at(b), b)

        guide_step(t)
        return carry

    def add(a, b):
        return (a.astype(F32) + b.astype(F32)).astype(BF16)

    loads["head_b"].wait()
    head_bt[...] = pad_lanes(head_b[...].T, 128)
    loads["proj_g"].wait()
    proj_gp[...] = pad_lanes(proj_g[...], HGP)
    loads["fcg"].wait()
    head_sum[...] = jnp.zeros_like(head_sum)
    seven(cots, cot_send, cot_recv).wait_recv()
    seven(means, mn_send, mn_recv).wait_recv()

    lax.fori_loop(0, UNITS + 7 * SKEW, tick, 0)
    for d in range(4, 8):
        consume(d)

    def rows(shard):
        return pl.ds(pl.multiple_of(shard * SHARD, 16), SHARD)

    def y_peer(n):
        return lax.rem(y + n, 4)

    def one_copy(c, n):
        p = y_peer(n)
        return remote(grad.at[c, rows(p)], ones.at[c, n - 1], one_send, one_recv.at[c], {"grp": zh4 + p})

    def z_copy(c):
        return remote(zed.at[c], zed_in.at[c], z_send, z_recv.at[c], dev_z)

    def back_copy(c, n):
        ref = final.at[c, rows(y)]
        return remote(ref, ref, g1_send, g1_recv.at[c], {"grp": zh4 + y_peer(n)})

    def three(c, send, recv):
        part = final.at[c, pl.ds(0, 3 * SHARD)]
        return remote(part, part, send, recv, dev_z)

    patch_rows = head_sum[pl.ds(pl.multiple_of(j * 8, 8), 8), :]
    spare = [patch_rows[:, 128 * q : 128 * q + 128] for q in range(NC)]
    spare = [
        jnp.concatenate(spare[0:4], axis=0),
        pad_rows(spare[4], 32),
    ] + [jnp.zeros((32, 128), F32)] * 3
    def guide_stats():
        loads["head_g"].wait()
        loads["mod_g"].wait()
        loads["res_g"].wait()
        mods = jnp.concatenate([mod_g[n, pl.ds(when, 1), :] for n in range(3)], axis=0)
        mods = pad_rows(pad_lanes(mods, 256), 128)
        for q in range(2):
            high = min(128, WG - 128 * q)
            turned = mods[:, 128 * q : 128 * q + 128].T[0:high]
            at = slice(128 * q, 128 * q + high)
            gate_g[at, :] = jnp.broadcast_to(turned[:, 0:1], (high, 128))
            shift_g[at, :] = jnp.broadcast_to(turned[:, 1:2], (high, 128))
            scale_g[at, :] = jnp.broadcast_to(1.0 + turned[:, 2:3], (high, 128))
        cot_g = ((1.0 - strength) * cot_ref[...]).astype(BF16)
        scaled_g[...] = (
            lax.dot_general(head_g[...], cot_g, (((0,), (0,)), ((), ())), preferred_element_type=F32)
            * scale_g[...]
        )
        term_g[...] = guide_term(j)
        for right_way in (True, False):
            place = j if right_way else 7 - j
            got = gotg_r if right_way else gotg_l

            @pl.when(place > 0)
            def _():
                guide_copy(right_way, 7 - place).wait_recv()
                term_g[...] += got[7 - place].astype(F32)

        stream = res_g[...].astype(F32) + gate_g[...] * term_g[...]
        mean_g = jnp.sum(stream, axis=0, keepdims=True) * (1.0 / WG)
        away_g = stream - mean_g
        dev_g[...] = away_g
        up_g = scaled_g[...]
        stats_g[me] = pad_rows(
            jnp.concatenate(
                [
                    mean_g,
                    jnp.sum(away_g * away_g, axis=0, keepdims=True),
                    jnp.sum(up_g, axis=0, keepdims=True),
                    jnp.sum(up_g * away_g, axis=0, keepdims=True),
                ],
                axis=0,
            ),
            8,
        )
        for n in range(1, 8):
            go(remote(stats_g.at[me], stats_g.at[me], sg_send, sg_recv, {"seq": seq_peer(n)}))

    own_at = place_of(j)

    def own_big():
        inverse, offset, slope, base = (facts[j, n : n + 1, :] for n in range(4))
        value = spread[own_at].astype(F32)
        own = inverse * scaled_b[j] - slope * value - base
        for q in range(NC):
            grad_res_b[:, 128 * q : 128 * q + 128] = own[128 * q : 128 * q + 128, :].T.astype(BF16)
        shaped = ((inverse * value + offset) * scale_b[...] + shift_b[...]).astype(BF16)
        made_b[...] = strength * jnp.dot(head_b[...], shaped, preferred_element_type=F32)
    def own_guide():
        seven(stats_g, sg_send, sg_recv).wait_recv()
        inverse, offset, slope, base = norm([stats_g[s] for s in range(8)], stats_g[me][0:1], float(WG), float(DG))
        grad_res_g[...] = (inverse * scaled_g[...] - slope * dev_g[...] - base).astype(BF16)
        shaped = ((inverse * dev_g[...] + offset) * scale_g[...] + shift_g[...]).astype(BF16)
        out_g = jnp.dot(head_g[...], shaped, preferred_element_type=F32)
        parts[me] = (made_b[...] + (1.0 - strength) * out_g).astype(BF16)
        for n in range(1, 8):
            go(remote(parts.at[me], parts.at[me], pt_send, pt_recv, {"seq": seq_peer(n)}))

    def settle():
        part = fc_all.at[pl.ds(0, 7), pl.ds(0, HB)]
        remote(part, part, fc_send, fc_recv.at[0, 0], {"seq": sib}).wait_send()
        part = fcg_all.at[pl.ds(0, 7), pl.ds(0, HG)]
        remote(part, part, fcg_send, fcg_recv.at[0], {"seq": sib}).wait_send()
        seven(cots, cot_send, cot_recv).wait_send()
        seven(means, mn_send, mn_recv).wait_send()
        for u in range(UNITS - DEPTH, UNITS):
            in_copy(jnp.int32(u // NQ), jnp.int32(u % NQ)).wait_send()

        @pl.when(place > 0)
        def _():
            remote(spread, spread, out_send, out_recv.at[0, 0], {"seq": sib}).wait_send()

        part = scaled_b.at[0, pl.ds(0, 7 * 8 * 8)]
        remote(part, part, st_send, st_recv.at[0], {"seq": sib}).wait_send()

        def drain(b, carry):
            for right_way in (True, False):

                @pl.when(b < (7 - j if right_way else j))
                def _():
                    guide_copy(right_way, b).wait_send()

            return carry

        lax.fori_loop(0, 7, drain, 0)

    def stage_grad(c):
        at = slice(128 * c, 128 * c + 128)
        grad[c, 0:HB, :] = lax.dot_general(
            jnp.concatenate([fc_all[s, 0:HB, :] for s in range(8)], axis=1),
            jnp.concatenate([signal[s, at, :] for s in range(8)], axis=1),
            (((1,), (1,)), ((), ())),
            preferred_element_type=F32,
        ).astype(BF16)
        grad[c, HB:HBP, :] = spare[c].astype(BF16)
        for n in (2, 1, 3):
            go(one_copy(c, n))

    def stage_one(c):
        three(c, one_send, one_recv.at[c]).wait_recv()
        total = grad[c, rows(y), :].astype(F32)
        for n in range(3):
            total += ones[c, n].astype(F32)
        zed[c] = total.astype(BF16)

    def stage_z(c):
        z_copy(c).wait_recv()
        final[c, rows(y), :] = add(zed[c], zed_in[c])
        for n in (2, 1, 3):
            go(back_copy(c, n))

    def stage_out(c):
        three(c, g1_send, g1_recv.at[c]).wait_recv()
        grad_proj_ref[:, 128 * c : 128 * c + 128] = final[c, 0:HB, :]
        if c == 1:
            heads[j, 0:32, :] = final[0, HB:HBP, :]
            heads[j, 32:64, :] = final[1, HB:HBP, :]
            for n in range(1, 8):
                go(remote(heads.at[j], heads.at[j], hd_send, hd_recv, {"tp": tp_peer(n)}))

    def predict():
        seven(parts, pt_send, pt_recv).wait_recv()
        guided_ref[...] = sum(parts[s].astype(F32) for s in range(8))

    def collect_heads():
        seven(heads, hd_send, hd_recv).wait_recv()
        for p in range(8):
            block = heads[p].astype(F32)
            for q in range(NC):
                grad_head_ref[8 * p : 8 * p + 8, 128 * q : 128 * q + 128] = block[8 * q : 8 * q + 8]

    def stage_across(c):
        go(z_copy(c))

    A, B, Z, C, D = stage_grad, stage_one, stage_across, stage_z, stage_out
    A(0)
    A(1)
    B(0)
    Z(0)
    A(2)
    B(1)
    Z(1)
    A(3)
    B(2)
    Z(2)
    A(4)
    B(3)
    guide_stats()
    B(4)
    own_big()
    C(0)
    Z(3)
    own_guide()
    C(1)
    Z(4)
    D(0)
    settle()
    C(2)
    D(1)
    predict()
    C(3)
    D(2)
    collect_heads()
    C(4)
    D(3)
    D(4)

    whole = final.at[:, pl.ds(0, 3 * SHARD)]
    remote(whole, whole, one_send, one_recv.at[0], dev_z).wait_send()
    remote(zed, zed_in, z_send, z_recv.at[0], dev_z).wait_send()
    remote(whole, whole, g1_send, g1_recv.at[0], dev_z).wait_send()
    seven(stats_g, sg_send, sg_recv).wait_send()
    seven(parts, pt_send, pt_recv).wait_send()
    seven(heads, hd_send, hd_recv).wait_send()


def shards(
    fc_big,
    fc_guide,
    res_big,
    res_guide,
    cotangent,
    proj_big,
    proj_guide,
    head_big,
    head_guide,
    modulation_big,
    modulation_guide,
    weight_table,
    time_index,
    weight_index,
):
    smem = pl.BlockSpec(memory_space=pltpu.SMEM)
    vmem = pl.BlockSpec(memory_space=pltpu.VMEM)
    hbm = pl.BlockSpec(memory_space=pl.ANY)
    dma = pltpu.SemaphoreType.DMA
    V = pltpu.VMEM
    shapes = (
        ((PATCH, TOK), F32),
        ((HB, WB), BF16),
        ((PATCH, WB), F32),
        ((TOK, WB), BF16),
        ((WG, TOK), BF16),
    )
    made = pl.pallas_call(
        kernel,
        out_shape=tuple(V(*s) for s in shapes),
        in_specs=[smem] * 3 + [hbm] * 11,
        out_specs=(vmem,) * 5,
        scratch_shapes=[
            V((TOK, WB), BF16),
            V((WG, TOK), BF16),
            V((PATCH, TOK), F32),
            V((HBP, WB), BF16),
            V((WG, HG), BF16),
            V((PATCH, WB), BF16),
            V((PATCH, WG), BF16),
            V((3, STEPS, WB), F32),
            V((3, STEPS, WG), F32),
            V((WB, HBP), BF16),
            V((WG, HGP), BF16),
            V((WB, 128), BF16),
            V((WB, 128), F32),
            V((WB, 128), F32),
            V((WB, 128), F32),
            V((WG, 128), F32),
            V((WG, 128), F32),
            V((WG, 128), F32),
            V((8, HBP, TOK), BF16),
            V((8, HGP, TOK), BF16),
            V((8, WB, TOK), F32),
            V((WG, TOK), F32),
            V((8, WB, TOK), BF16),
            V((8, WB, TOK), BF16),
            V((8, WB, TOK), BF16),
            V((8, 8, TOK), F32),
            V((7, WG, TOK), BF16),
            V((7, WG, TOK), BF16),
            V((7, WG, TOK), BF16),
            V((7, WG, TOK), BF16),
            V((WB, TOK), F32),
            V((WG, TOK), F32),
            V((8, WB, TOK), F32),
            V((WG, TOK), F32),
            V((8, WB, TOK), BF16),
            V((8, PATCH, TOK), BF16),
            V((8, 8, 8, TOK), F32),
            V((8, 8, TOK), F32),
            V((8, 8, TOK), F32),
            V((8, WB, TOK), BF16),
            V((PATCH, WB), F32),
            V((8, PATCH, TOK), BF16),
            V((NC, HBP, 128), BF16),
            V((NC, 3, SHARD, 128), BF16),
            V((NC, SHARD, 128), BF16),
            V((NC, SHARD, 128), BF16),
            V((NC, HBP, 128), BF16),
            V((8, 64, 128), BF16),
            V((PATCH, TOK), F32),
            dma((11,)),
            dma(()),
            dma((8, 2)),
            dma(()),
            dma((8,)),
            dma(()),
            dma(()),
            dma(()),
            dma(()),
            dma((DEPTH,)),
            dma((8, NQ)),
            dma(()),
            dma((8, NQ)),
            dma((7,)),
            dma((7,)),
            dma((7,)),
            dma((7,)),
            dma(()),
            dma((8,)),
            dma(()),
            dma(()),
            dma(()),
            dma(()),
            dma(()),
            dma((NC,)),
            dma(()),
            dma((NC,)),
            dma(()),
            dma((NC,)),
            dma(()),
            dma(()),
        ],
        compiler_params=pltpu.CompilerParams(
            collective_id=0, has_side_effects=True, vmem_limit_bytes=56 * 2**20
        ),
    )(
        time_index,
        weight_index,
        weight_table,
        fc_big.T,
        fc_guide.T,
        res_big,
        res_guide.T,
        cotangent.T,
        proj_big,
        proj_guide.T,
        head_big.T,
        head_guide.T,
        modulation_big.transpose(1, 0, 2),
        modulation_guide.transpose(1, 0, 2),
    )
    guided, grad_proj, grad_head, grad_res_big, grad_res_guide = made
    return guided.T, grad_proj, grad_head.T, grad_res_big, grad_res_guide.T


def solution(mesh):
    placed = (
        P(("grp", "seq"), "tp"),
        P(("grp", "seq"), "tp"),
        P(("grp", "tp"), "seq"),
        P(("grp", "tp"), "seq"),
        P(("grp", "tp"), None),
        P("tp", "seq"),
        P("tp", "seq"),
        P("seq", None),
        P("seq", None),
        P(None, None, "seq"),
        P(None, None, "seq"),
        P(),
        P("grp"),
        P("grp"),
    )
    return jax.shard_map(
        shards,
        mesh=mesh,
        in_specs=placed,
        out_specs=(
            P(("grp", "tp"), None),
            P("tp", "seq"),
            P("seq", None),
            P(("grp", "tp"), "seq"),
            P(("grp", "tp"), "seq"),
        ),
        check_vma=False,
    )
```

```python
import jax
import jax.numpy as jnp
from jax import lax
from jax.experimental import pallas as pl
from jax.experimental.pallas import tpu as pltpu
from jax.sharding import PartitionSpec as P

MESH = pl.DeviceIdType.MESH
F32 = jnp.float32
BF16 = jnp.bfloat16

DB = 5120
DG = 1536
EPSILON = 1e-06

TOK = 128
WB = 640
WG = 192
HB = 864
HBP = 896
HG = 560
HGP = 640
PATCH = 64
STEPS = 50
NQ = 5
SUB = WB // NQ
UNITS = 8 * NQ
SKEW = 5
DEPTH = 3
GSTEP = 2
NC = 5
SHARD = 224


def remote(src, dst, send, recv, device):
    return pltpu.make_async_remote_copy(
        src_ref=src, dst_ref=dst, send_sem=send, recv_sem=recv, device_id=device, device_id_type=MESH
    )


def kernel(
    time_ref,
    level_ref,
    table_ref,
    fc_b,
    fc_g,
    res_b_in,
    res_g_in,
    cot_in,
    proj_b_in,
    proj_g_in,
    head_b_in,
    head_g_in,
    mod_b_in,
    mod_g_in,
    guided_ref,
    grad_proj_ref,
    grad_head_ref,
    grad_res_b,
    grad_res_g,
    res_b,
    res_g,
    cot_ref,
    proj_b,
    proj_g,
    head_b,
    head_g,
    mod_b,
    mod_g,
    proj_bt,
    proj_gp,
    head_bt,
    gate_b,
    shift_b,
    scale_b,
    gate_g,
    shift_g,
    scale_g,
    fc_all,
    fcg_all,
    term,
    term_g,
    got,
    put,
    cross,
    means,
    gotg_r,
    gotg_l,
    putg_r,
    putg_l,
    dev_b,
    dev_g,
    scaled_b,
    scaled_g,
    spread,
    cots,
    stats,
    stats_g,
    facts,
    signal,
    head_sum,
    parts,
    grad,
    ones,
    zed,
    zed_in,
    final,
    heads,
    made_b,
    in_sem,
    fc_send,
    fc_recv,
    fcg_send,
    fcg_recv,
    cot_send,
    cot_recv,
    mn_send,
    mn_recv,
    in_send,
    in_recv,
    out_send,
    out_recv,
    rg_send,
    rg_recv,
    lg_send,
    lg_recv,
    st_send,
    st_recv,
    sg_send,
    sg_recv,
    pt_send,
    pt_recv,
    one_send,
    one_recv,
    z_send,
    z_recv,
    g1_send,
    g1_recv,
    hd_send,
    hd_recv,
):
    grp = lax.axis_index("grp")
    me = lax.axis_index("seq")
    j = lax.axis_index("tp")
    y = lax.rem(grp, 4)
    zh4 = grp - y
    x = lax.div(me, 2)
    core = lax.rem(me, 2)
    sib = me + 1 - 2 * core
    xr = lax.rem(x + 1, 4)
    xl = lax.rem(x + 3, 4)
    xf = lax.rem(x + 2, 4)
    dev_z = {"grp": lax.rem(grp + 4, 8)}

    def seq_peer(n):
        return lax.rem(me + n, 8)

    def tp_peer(n):
        return lax.rem(j + n, 8)

    barrier = pltpu.get_barrier_semaphore()
    for n in range(1, 8):
        pl.semaphore_signal(barrier, inc=1, device_id={"seq": seq_peer(n)}, device_id_type=MESH)
        pl.semaphore_signal(barrier, inc=1, device_id={"tp": tp_peer(n)}, device_id_type=MESH)
    for n in range(1, 4):
        device = {"grp": zh4 + lax.rem(y + n, 4)}
        pl.semaphore_signal(barrier, inc=1, device_id=device, device_id_type=MESH)
    pl.semaphore_signal(barrier, inc=1, device_id=dev_z, device_id_type=MESH)

    loads = {}
    for n, (name, src, dst) in enumerate(
        (
            ("mod_b", mod_b_in, mod_b),
            ("res_b", res_b_in, res_b),
            ("proj_b", proj_b_in, proj_b.at[pl.ds(0, HB)]),
            ("fc", fc_b, fc_all.at[me, pl.ds(0, HB)]),
            ("cot", cot_in, cot_ref),
            ("head_b", head_b_in, head_b),
            ("fcg", fc_g, fcg_all.at[me, pl.ds(0, HG)]),
            ("proj_g", proj_g_in, proj_g),
            ("head_g", head_g_in, head_g),
            ("mod_g", mod_g_in, mod_g),
            ("res_g", res_g_in, res_g),
        )
    ):
        loads[name] = pltpu.make_async_copy(src, dst, in_sem.at[n])
        loads[name].start()

    strength = table_ref[level_ref[0]]
    when = time_ref[0]
    pl.semaphore_wait(barrier, 18)

    def half(h):
        return pl.ds(h * (HB // 2), HB // 2)

    def hidden(s, h):
        return fc_all.at[s, half(h)]

    def seven(ref, send, recv):
        part = ref.at[pl.ds(0, 7)]
        return remote(part, part, send, recv, {"seq": sib})

    def hidden_copy(s, h, k, target, src=None):
        return remote(
            hidden(s, h) if src is None else src.at[half(h)], hidden(s, h), fc_send, fc_recv.at[s, h], {"seq": target}
        )

    to_r, to_l = 2 * xr + core, 2 * xl + core

    def go(copy):
        copy.start()

    def send_hidden(s, h, k, target, src=None):
        go(hidden_copy(s, h, k, target, src))

    def wait_hidden(s, h):
        hidden_copy(s, h, 0, sib).wait_recv()

    send_hidden(me, 0, 0, to_r, fc_b)
    send_hidden(me, 1, 1, to_l, fc_b)
    send_hidden(me, 0, 2, sib, fc_b)
    send_hidden(me, 1, 3, sib, fc_b)
    send_hidden(me, 1, 4, to_r, fc_b)
    send_hidden(me, 0, 5, to_l, fc_b)

    def pad_rows(value, rows):
        return jnp.concatenate([value, jnp.zeros((rows - value.shape[0], value.shape[1]), value.dtype)], axis=0)

    def pad_lanes(value, lanes):
        return jnp.concatenate([value, jnp.zeros((value.shape[0], lanes - value.shape[1]), value.dtype)], axis=1)

    for s in range(8):
        fc_all[s, HB:HBP, :] = jnp.zeros((HBP - HB, TOK), BF16)
    proj_b[HB:HBP, :] = jnp.zeros((HBP - HB, WB), BF16)
    loads["mod_b"].wait()
    mods = pad_rows(
        jnp.concatenate([mod_b[n, pl.ds(when, 1), :] for n in range(3)], axis=0), 128
    )
    loads["res_b"].wait()
    for q in range(NC):
        turned = mods[:, 128 * q : 128 * q + 128].T
        at = slice(128 * q, 128 * q + 128)
        gate_b[at, :] = jnp.broadcast_to(turned[:, 0:1], (128, 128))
        shift_b[at, :] = jnp.broadcast_to(turned[:, 1:2], (128, 128))
        scale_b[at, :] = jnp.broadcast_to(1.0 + turned[:, 2:3], (128, 128))
        dev_b[at, :] = res_b[:, at].astype(F32).T
    mean = jnp.sum(dev_b[...], axis=0, keepdims=True) * (1.0 / WB)
    dev_b[...] -= mean
    means[j] = jnp.broadcast_to(mean, (8, TOK))
    loads["proj_b"].wait()
    for q in range(NC):
        proj_bt[128 * q : 128 * q + 128, :] = proj_b[:, 128 * q : 128 * q + 128].T
    loads["fc"].wait()

    def terms(s):
        term[s] = gate_b[...] * jnp.dot(proj_bt[...], fc_all[s], preferred_element_type=F32)

        @pl.when(s == j)
        def _():
            term[s] += dev_b[...]

    left, right, far = to_l, to_r, 2 * xf + core
    left_s, right_s, far_s = 2 * xl + 1 - core, 2 * xr + 1 - core, 2 * xf + 1 - core

    pairs = (
        x,
        1 - lax.rem(x, 2),
        jnp.where(x < 2, 2, x - 2),
        jnp.where(x == 3, 2, 3),
    )

    def block_at(b):
        n = lax.div(b, 2)
        pair = jnp.where(n == 0, pairs[0], jnp.where(n == 1, pairs[1], jnp.where(n == 2, pairs[2], pairs[3])))
        return 2 * pair + jnp.where(lax.rem(b, 2) == 0, core, 1 - core)

    def place_of(d):
        return sum(jnp.where(block_at(jnp.int32(b)) == d, b, 0) for b in range(8))

    terms(me)

    def fcg_copy(s, n, target, src):
        return remote(src, fcg_all.at[s, pl.ds(0, HG)], fcg_send, fcg_recv.at[s], {"seq": target})

    relays = (
        (left, 0, 6, to_r),
        (left, 0, 7, sib),
        (right, 1, 8, to_l),
        (right, 1, 9, sib),
        (left, 1, 10, sib),
        (right, 0, 11, sib),
        (far, 0, 12, sib),
        (far, 1, 13, sib),
    )

    def relay(n):
        s, h, k, target = relays[n]
        hidden_copy(s, h, k, target).start()

    def scale_all():
        seven(cots, cot_send, cot_recv).wait_recv()
        seven(means, mn_send, mn_recv).wait_recv()

        def one(d, carry):
            scaled_b[d] = (
                jnp.dot(head_bt[...], pad_rows(cots[d], 128), preferred_element_type=F32) * scale_b[...]
            )
            return carry

        lax.fori_loop(0, 8, one, 0)

    def beside():
        wait_hidden(sib, 0)
        wait_hidden(sib, 1)

    def near():
        wait_hidden(left, 0)
        relay(0)
        relay(1)
        wait_hidden(right, 1)
        relay(2)
        relay(3)

    def near_rest():
        wait_hidden(left, 1)
        relay(4)
        wait_hidden(right, 0)
        relay(5)

    def near_others():
        for h in range(2):
            wait_hidden(left_s, h)
            wait_hidden(right_s, h)

    def opposite():
        wait_hidden(far, 0)
        relay(6)
        wait_hidden(far, 1)
        relay(7)

    def opposite_others():
        wait_hidden(far_s, 0)
        wait_hidden(far_s, 1)
        for n in range(1, 8):
            fcg_copy(me, n, seq_peer(n), fc_g).start()

    def share():
        loads["cot"].wait()
        cot = cot_ref[...]
        cots[j] = (strength * cot).astype(BF16)
        for n in range(1, 8):
            go(remote(cots.at[j], cots.at[j], cot_send, cot_recv, {"tp": tp_peer(n)}))
        for n in range(1, 8):
            go(remote(means.at[j], means.at[j], mn_send, mn_recv, {"tp": tp_peer(n)}))

    def prepare():
        for s in range(8):
            fcg_all[s, HG:HGP, :] = jnp.zeros((HGP - HG, TOK), BF16)
        loads["head_b"].wait()
        head_bt[...] = pad_lanes(head_b[...].T, 128)
        loads["proj_g"].wait()
        proj_gp[...] = pad_lanes(proj_g[...], HGP)
        loads["fcg"].wait()
        head_sum[...] = jnp.zeros_like(head_sum)

    events = (
        (1, share),
        (3, prepare),
        (NQ, beside),
        (2 * NQ - 2, near),
        (2 * NQ, near_rest),
        (2 * NQ + 2, scale_all),
        (3 * NQ, near_others),
        (4 * NQ - 2, opposite),
        (5 * NQ, opposite_others),
    )

    in_left = j < 4
    place = jnp.where(in_left, j, 7 - j)
    toward = {"tp": jnp.where(in_left, j + 1, j - 1)}
    away = {"tp": jnp.where(in_left, j - 1, j + 1)}

    def piece(q):
        return pl.ds(pl.multiple_of(q * SUB, 16), SUB)

    def in_copy(b, q):
        return remote(put.at[b, piece(q)], got.at[b, piece(q)], in_send.at[lax.rem(b * NQ + q, DEPTH)], in_recv.at[b, q], toward)

    def cross_copy(b, q):
        return remote(put.at[b, piece(q)], cross.at[b, piece(q)], in_send.at[lax.rem(b * NQ + q, DEPTH)], out_recv.at[b, q], toward)

    def out_copy(b, q):
        ref = spread.at[b, piece(q)]
        return remote(ref, ref, out_send, out_recv.at[b, q], away)

    def stat_copy(s, n, d, target):
        ref = stats.at[d, s]
        return remote(ref, ref, st_send, st_recv.at[d], {"seq": target})

    def block_stats(d, b):
        up = scaled_b[d]
        value = spread[b].astype(F32)
        mean = jnp.sum(value, axis=0, keepdims=True) * (1.0 / WB)
        value -= mean
        stats[d, me] = pad_rows(
            jnp.concatenate(
                [
                    means[d, 0:1] + mean,
                    jnp.sum(value * value, axis=0, keepdims=True),
                    jnp.sum(up, axis=0, keepdims=True),
                    jnp.sum(up * value, axis=0, keepdims=True),
                ],
                axis=0,
            ),
            8,
        )
        for n in range(1, 8):
            stat_copy(me, n, d, seq_peer(n)).start()

    def norm(every, mine, width, whole):
        centre = sum(r[0:1] for r in every) * (1.0 / 8)
        gaps = [r[0:1] - centre for r in every]
        square_sum = sum(r[1:2] + width * (g * g) for r, g in zip(every, gaps))
        inverse = lax.rsqrt(square_sum * (1.0 / whole) + EPSILON)
        first = sum(r[2:3] for r in every) * (1.0 / whole)
        cross_sum = sum(r[3:4] + r[2:3] * g for r, g in zip(every, gaps))
        second = inverse * cross_sum * (1.0 / whole)
        offset = inverse * (mine - centre)
        return inverse, offset, inverse * inverse * second, inverse * (first + offset * second)

    def consume(d):
        b = place_of(d)
        seven(stats.at[d], st_send, st_recv.at[d]).wait_recv()
        every = [stats[d, s] for s in range(8)]
        inverse, offset, slope, base = norm(every, means[d, 0:1], float(WB), float(DB))
        facts[d] = pad_rows(jnp.concatenate([inverse, offset, slope, base], axis=0), 8)
        value = spread[b].astype(F32)
        signal[d] = (
            gate_b[...] * (inverse * scaled_b[d] - slope * value - base)
        ).astype(BF16)
        shaped = ((inverse * value + offset) * scale_b[...] + shift_b[...]).astype(BF16)
        head_sum[...] += lax.dot_general(
            cots[d], shaped, (((1,), (1,)), ((), ())), preferred_element_type=F32
        )

    def guide_copy(right_way, i):
        if right_way:
            return remote(putg_r.at[i], gotg_r.at[i], rg_send.at[i], rg_recv.at[i], {"tp": j + 1})
        return remote(putg_l.at[i], gotg_l.at[i], lg_send.at[i], lg_recv.at[i], {"tp": j - 1})

    def guide_term(s):
        @pl.when(s != me)
        def _():
            fcg_copy(s, 0, s, fcg_all.at[s, pl.ds(0, HG)]).wait_recv()

        return jnp.dot(proj_gp[...], fcg_all[s], preferred_element_type=F32)

    def guide_step(t):
        for right_way in (True, False):
            far_end = j if right_way else 7 - j
            w = t - UNITS - SKEW * far_end
            i = lax.div(w, GSTEP)
            put, got = (putg_r, gotg_r) if right_way else (putg_l, gotg_l)

            @pl.when((w >= 0) & (lax.rem(w, GSTEP) == 0) & (i < 7 - far_end))
            def _():
                own = guide_term(7 - i if right_way else i)

                @pl.when(far_end > 0)
                def _():
                    guide_copy(right_way, i).wait_recv()
                    put[i] = (got[i].astype(F32) + own).astype(BF16)

                @pl.when(far_end == 0)
                def _():
                    put[i] = own.astype(BF16)

                guide_copy(right_way, i).start()

    def tick(t, carry):
        for at, action in events:
            pl.when(t == at)(action)

        @pl.when((lax.rem(t, NQ) == 0) & (t > 0) & (t < UNITS))
        def _():
            terms(block_at(lax.div(t, NQ)))

        u = t - SKEW * place

        @pl.when((u >= 0) & (u < UNITS))
        def _():
            b = lax.div(u, NQ)
            q = lax.rem(u, NQ)
            own = term[block_at(b), piece(q), :]

            @pl.when(place > 0)
            def _():
                in_copy(b, q).wait_recv()
                put[b, piece(q), :] = (got[b, piece(q), :].astype(F32) + own).astype(BF16)

            @pl.when(place == 0)
            def _():
                put[b, piece(q), :] = own.astype(BF16)

            @pl.when(u >= DEPTH)
            def _():
                in_copy(b, q).wait_send()

            @pl.when(place < 3)
            def _():
                in_copy(b, q).start()

            @pl.when(place == 3)
            def _():
                cross_copy(b, q).start()

        v = t - SKEW * (7 - place)

        @pl.when((v >= 0) & (v < UNITS))
        def _():
            b = lax.div(v, NQ)
            q = lax.rem(v, NQ)

            @pl.when(place == 3)
            def _():
                cross_copy(b, q).wait_recv()
                spread[b, piece(q), :] = add(put[b, piece(q), :], cross[b, piece(q), :])

            @pl.when(place < 3)
            def _():
                out_copy(b, q).wait_recv()

            @pl.when(place > 0)
            def _():
                out_copy(b, q).start()

            @pl.when(q == NQ - 1)
            def _():
                block_stats(block_at(b), b)

        guide_step(t)
        return carry

    def add(a, b):
        return (a.astype(F32) + b.astype(F32)).astype(BF16)

    lax.fori_loop(0, UNITS + 7 * SKEW, tick, 0)
    def consume_one(d, carry):
        consume(d)
        return carry

    lax.fori_loop(0, 8, consume_one, 0)

    def rows(shard):
        return pl.ds(pl.multiple_of(shard * SHARD, 16), SHARD)

    def y_peer(n):
        return lax.rem(y + n, 4)

    def one_copy(c, n):
        p = y_peer(n)
        return remote(grad.at[c, rows(p)], ones.at[c, n - 1], one_send, one_recv.at[c], {"grp": zh4 + p})

    def z_copy(c):
        return remote(zed.at[c], zed_in.at[c], z_send, z_recv.at[c], dev_z)

    def back_copy(c, n):
        ref = final.at[c, rows(y)]
        return remote(ref, ref, g1_send, g1_recv.at[c], {"grp": zh4 + y_peer(n)})

    def three(c, send, recv):
        part = final.at[c, pl.ds(0, 3 * SHARD)]
        return remote(part, part, send, recv, dev_z)

    patch_rows = head_sum[pl.ds(pl.multiple_of(j * 8, 8), 8), :]
    spare = [patch_rows[:, 128 * q : 128 * q + 128] for q in range(NC)]
    spare = [
        jnp.concatenate(spare[0:4], axis=0),
        pad_rows(spare[4], 32),
    ] + [jnp.zeros((32, 128), F32)] * 3
    def guide_stats():
        loads["head_g"].wait()
        loads["mod_g"].wait()
        loads["res_g"].wait()
        mods = jnp.concatenate([mod_g[n, pl.ds(when, 1), :] for n in range(3)], axis=0)
        mods = pad_rows(pad_lanes(mods, 256), 128)
        for q in range(2):
            high = min(128, WG - 128 * q)
            turned = mods[:, 128 * q : 128 * q + 128].T[0:high]
            at = slice(128 * q, 128 * q + high)
            gate_g[at, :] = jnp.broadcast_to(turned[:, 0:1], (high, 128))
            shift_g[at, :] = jnp.broadcast_to(turned[:, 1:2], (high, 128))
            scale_g[at, :] = jnp.broadcast_to(1.0 + turned[:, 2:3], (high, 128))
        cot_g = ((1.0 - strength) * cot_ref[...]).astype(BF16)
        scaled_g[...] = (
            lax.dot_general(head_g[...], cot_g, (((0,), (0,)), ((), ())), preferred_element_type=F32)
            * scale_g[...]
        )
        term_g[...] = guide_term(j)
        for right_way in (True, False):
            place = j if right_way else 7 - j
            got = gotg_r if right_way else gotg_l

            @pl.when(place > 0)
            def _():
                guide_copy(right_way, 7 - place).wait_recv()
                term_g[...] += got[7 - place].astype(F32)

        stream = res_g[...].astype(F32) + gate_g[...] * term_g[...]
        mean_g = jnp.sum(stream, axis=0, keepdims=True) * (1.0 / WG)
        away_g = stream - mean_g
        dev_g[...] = away_g
        up_g = scaled_g[...]
        stats_g[me] = pad_rows(
            jnp.concatenate(
                [
                    mean_g,
                    jnp.sum(away_g * away_g, axis=0, keepdims=True),
                    jnp.sum(up_g, axis=0, keepdims=True),
                    jnp.sum(up_g * away_g, axis=0, keepdims=True),
                ],
                axis=0,
            ),
            8,
        )
        for n in range(1, 8):
            go(remote(stats_g.at[me], stats_g.at[me], sg_send, sg_recv, {"seq": seq_peer(n)}))

    own_at = place_of(j)

    def own_big():
        inverse, offset, slope, base = (facts[j, n : n + 1, :] for n in range(4))
        value = spread[own_at].astype(F32)
        own = inverse * scaled_b[j] - slope * value - base
        for q in range(NC):
            grad_res_b[:, 128 * q : 128 * q + 128] = own[128 * q : 128 * q + 128, :].T.astype(BF16)
        shaped = ((inverse * value + offset) * scale_b[...] + shift_b[...]).astype(BF16)
        made_b[...] = strength * jnp.dot(head_b[...], shaped, preferred_element_type=F32)
    def own_guide():
        seven(stats_g, sg_send, sg_recv).wait_recv()
        inverse, offset, slope, base = norm([stats_g[s] for s in range(8)], stats_g[me][0:1], float(WG), float(DG))
        grad_res_g[...] = (inverse * scaled_g[...] - slope * dev_g[...] - base).astype(BF16)
        shaped = ((inverse * dev_g[...] + offset) * scale_g[...] + shift_g[...]).astype(BF16)
        out_g = jnp.dot(head_g[...], shaped, preferred_element_type=F32)
        parts[me] = (made_b[...] + (1.0 - strength) * out_g).astype(BF16)
        for n in range(1, 8):
            go(remote(parts.at[me], parts.at[me], pt_send, pt_recv, {"seq": seq_peer(n)}))

    def settle():
        part = fc_all.at[pl.ds(0, 7), pl.ds(0, HB)]
        remote(part, part, fc_send, fc_recv.at[0, 0], {"seq": sib}).wait_send()
        part = fcg_all.at[pl.ds(0, 7), pl.ds(0, HG)]
        remote(part, part, fcg_send, fcg_recv.at[0], {"seq": sib}).wait_send()
        seven(cots, cot_send, cot_recv).wait_send()
        seven(means, mn_send, mn_recv).wait_send()
        for u in range(UNITS - DEPTH, UNITS):
            in_copy(jnp.int32(u // NQ), jnp.int32(u % NQ)).wait_send()

        @pl.when(place > 0)
        def _():
            remote(spread, spread, out_send, out_recv.at[0, 0], {"seq": sib}).wait_send()

        part = scaled_b.at[0, pl.ds(0, 7 * 8 * 8)]
        remote(part, part, st_send, st_recv.at[0], {"seq": sib}).wait_send()

        def drain(b, carry):
            for right_way in (True, False):

                @pl.when(b < (7 - j if right_way else j))
                def _():
                    guide_copy(right_way, b).wait_send()

            return carry

        lax.fori_loop(0, 7, drain, 0)

    def stage_grad(c):
        at = slice(128 * c, 128 * c + 128)
        grad[c, 0:HB, :] = lax.dot_general(
            jnp.concatenate([fc_all[s, 0:HB, :] for s in range(8)], axis=1),
            jnp.concatenate([signal[s, at, :] for s in range(8)], axis=1),
            (((1,), (1,)), ((), ())),
            preferred_element_type=F32,
        ).astype(BF16)
        grad[c, HB:HBP, :] = spare[c].astype(BF16)
        for n in (2, 1, 3):
            go(one_copy(c, n))

    def stage_one(c):
        three(c, one_send, one_recv.at[c]).wait_recv()
        total = grad[c, rows(y), :].astype(F32)
        for n in range(3):
            total += ones[c, n].astype(F32)
        zed[c] = total.astype(BF16)

    def stage_z(c):
        z_copy(c).wait_recv()
        final[c, rows(y), :] = add(zed[c], zed_in[c])
        for n in (2, 1, 3):
            go(back_copy(c, n))

    def stage_out(c):
        three(c, g1_send, g1_recv.at[c]).wait_recv()
        grad_proj_ref[:, 128 * c : 128 * c + 128] = final[c, 0:HB, :]
        if c == 1:
            heads[j, 0:32, :] = final[0, HB:HBP, :]
            heads[j, 32:64, :] = final[1, HB:HBP, :]
            for n in range(1, 8):
                go(remote(heads.at[j], heads.at[j], hd_send, hd_recv, {"tp": tp_peer(n)}))

    def predict():
        seven(parts, pt_send, pt_recv).wait_recv()
        guided_ref[...] = sum(parts[s].astype(F32) for s in range(8))

    def collect_heads():
        seven(heads, hd_send, hd_recv).wait_recv()
        for p in range(8):
            block = heads[p].astype(F32)
            for q in range(NC):
                grad_head_ref[8 * p : 8 * p + 8, 128 * q : 128 * q + 128] = block[8 * q : 8 * q + 8]

    def stage_across(c):
        go(z_copy(c))

    A, B, Z, C, D = stage_grad, stage_one, stage_across, stage_z, stage_out
    A(0)
    A(1)
    B(0)
    Z(0)
    A(2)
    B(1)
    Z(1)
    A(3)
    B(2)
    Z(2)
    A(4)
    B(3)
    guide_stats()
    B(4)
    own_big()
    C(0)
    Z(3)
    own_guide()
    C(1)
    Z(4)
    D(0)
    settle()
    C(2)
    D(1)
    predict()
    C(3)
    D(2)
    collect_heads()
    C(4)
    D(3)
    D(4)

    whole = final.at[:, pl.ds(0, 3 * SHARD)]
    remote(whole, whole, one_send, one_recv.at[0], dev_z).wait_send()
    remote(zed, zed_in, z_send, z_recv.at[0], dev_z).wait_send()
    remote(whole, whole, g1_send, g1_recv.at[0], dev_z).wait_send()
    seven(stats_g, sg_send, sg_recv).wait_send()
    seven(parts, pt_send, pt_recv).wait_send()
    seven(heads, hd_send, hd_recv).wait_send()


def shards(
    fc_big,
    fc_guide,
    res_big,
    res_guide,
    cotangent,
    proj_big,
    proj_guide,
    head_big,
    head_guide,
    modulation_big,
    modulation_guide,
    weight_table,
    time_index,
    weight_index,
):
    smem = pl.BlockSpec(memory_space=pltpu.SMEM)
    vmem = pl.BlockSpec(memory_space=pltpu.VMEM)
    hbm = pl.BlockSpec(memory_space=pl.ANY)
    dma = pltpu.SemaphoreType.DMA
    V = pltpu.VMEM
    shapes = (
        ((PATCH, TOK), F32),
        ((HB, WB), BF16),
        ((PATCH, WB), F32),
        ((TOK, WB), BF16),
        ((WG, TOK), BF16),
    )
    made = pl.pallas_call(
        kernel,
        out_shape=tuple(V(*s) for s in shapes),
        in_specs=[smem] * 3 + [hbm] * 11,
        out_specs=(vmem,) * 5,
        scratch_shapes=[
            V((TOK, WB), BF16),
            V((WG, TOK), BF16),
            V((PATCH, TOK), F32),
            V((HBP, WB), BF16),
            V((WG, HG), BF16),
            V((PATCH, WB), BF16),
            V((PATCH, WG), BF16),
            V((3, STEPS, WB), F32),
            V((3, STEPS, WG), F32),
            V((WB, HBP), BF16),
            V((WG, HGP), BF16),
            V((WB, 128), BF16),
            V((WB, 128), F32),
            V((WB, 128), F32),
            V((WB, 128), F32),
            V((WG, 128), F32),
            V((WG, 128), F32),
            V((WG, 128), F32),
            V((8, HBP, TOK), BF16),
            V((8, HGP, TOK), BF16),
            V((8, WB, TOK), F32),
            V((WG, TOK), F32),
            V((8, WB, TOK), BF16),
            V((8, WB, TOK), BF16),
            V((8, WB, TOK), BF16),
            V((8, 8, TOK), F32),
            V((7, WG, TOK), BF16),
            V((7, WG, TOK), BF16),
            V((7, WG, TOK), BF16),
            V((7, WG, TOK), BF16),
            V((WB, TOK), F32),
            V((WG, TOK), F32),
            V((8, WB, TOK), F32),
            V((WG, TOK), F32),
            V((8, WB, TOK), BF16),
            V((8, PATCH, TOK), BF16),
            V((8, 8, 8, TOK), F32),
            V((8, 8, TOK), F32),
            V((8, 8, TOK), F32),
            V((8, WB, TOK), BF16),
            V((PATCH, WB), F32),
            V((8, PATCH, TOK), BF16),
            V((NC, HBP, 128), BF16),
            V((NC, 3, SHARD, 128), BF16),
            V((NC, SHARD, 128), BF16),
            V((NC, SHARD, 128), BF16),
            V((NC, HBP, 128), BF16),
            V((8, 64, 128), BF16),
            V((PATCH, TOK), F32),
            dma((11,)),
            dma(()),
            dma((8, 2)),
            dma(()),
            dma((8,)),
            dma(()),
            dma(()),
            dma(()),
            dma(()),
            dma((DEPTH,)),
            dma((8, NQ)),
            dma(()),
            dma((8, NQ)),
            dma((7,)),
            dma((7,)),
            dma((7,)),
            dma((7,)),
            dma(()),
            dma((8,)),
            dma(()),
            dma(()),
            dma(()),
            dma(()),
            dma(()),
            dma((NC,)),
            dma(()),
            dma((NC,)),
            dma(()),
            dma((NC,)),
            dma(()),
            dma(()),
        ],
        compiler_params=pltpu.CompilerParams(
            collective_id=0, has_side_effects=True, vmem_limit_bytes=56 * 2**20
        ),
    )(
        time_index,
        weight_index,
        weight_table,
        fc_big.T,
        fc_guide.T,
        res_big,
        res_guide.T,
        cotangent.T,
        proj_big,
        proj_guide.T,
        head_big.T,
        head_guide.T,
        modulation_big.transpose(1, 0, 2),
        modulation_guide.transpose(1, 0, 2),
    )
    guided, grad_proj, grad_head, grad_res_big, grad_res_guide = made
    return guided.T, grad_proj, grad_head.T, grad_res_big, grad_res_guide.T


def solution(mesh):
    placed = (
        P(("grp", "seq"), "tp"),
        P(("grp", "seq"), "tp"),
        P(("grp", "tp"), "seq"),
        P(("grp", "tp"), "seq"),
        P(("grp", "tp"), None),
        P("tp", "seq"),
        P("tp", "seq"),
        P("seq", None),
        P("seq", None),
        P(None, None, "seq"),
        P(None, None, "seq"),
        P(),
        P("grp"),
        P("grp"),
    )
    return jax.shard_map(
        shards,
        mesh=mesh,
        in_specs=placed,
        out_specs=(
            P(("grp", "tp"), None),
            P("tp", "seq"),
            P("seq", None),
            P(("grp", "tp"), "seq"),
            P(("grp", "tp"), "seq"),
        ),
        check_vma=False,
    )
```
